128 devices in a mesh: ty: 16 (over y, z_lo, core), tx: 8 (over z_hi, x).
Axes of the slice: x: 4, y: 4, z: 4 (z_hi: 2, z_lo: 2; z = z_hi * 2 + z_lo), core: 2. Of those that a mesh axis runs over, the one named last changes fastest.
Arguments:
- residual: float32 [128, 4, 128, 768], P(('ty', 'tx')), may hold values from -6 to 6
- counts: int32 [128, 128], P(('ty', 'tx')), may hold values from 96 to 768, as said below
- offsets: int32 [128, 2, 128, 768], P(('ty', 'tx')), may hold values from 2 to 122
- positions: float32 [128, 2, 128, 768], P(('ty', 'tx')), may hold values from 0 to 1
- coef_fine: float32 [4, 2048, 1024], P(None, 'ty', 'tx'), may hold values from -0.4 to 0.4
- coef_coarse: float32 [4, 1024, 512], P(None, 'ty', 'tx'), may hold values from -0.4 to 0.4
- kappa_map: int32 [2048, 1024], P('ty', 'tx'), may hold values from 0 to 7
- kappa_table: float32 [2, 8], replicated, may hold values from 0.05 to 3
- level_weight: float32 [2], replicated, may hold values from 0.5 to 2
Outputs:
- fine_grad: float32 [4, 2048, 1024], P(None, 'ty', 'tx')
- coarse_grad: float32 [4, 1024, 512], P(None, 'ty', 'tx')
The draws below stay inside these ranges and needn't reach their ends.
Inputs may be any that keep to these rules, and one draw needn't show every extreme that they name: counts[s, d] is the number of live leading rows in the bin from tile s to tile d; in every draw some destination tiles receive 768 live rows from every source. offsets keep every row's 4 x 4 fine patch and 4 x 4 coarse patch inside its destination tile.
All inputs are finite; a program needn't handle non-finite values.
Results may differ from the reference program's by a relative error of at most 0.0032.
Values sent between devices are 32-bit elements; how exact they have to be, the bound alone decides.
No kernel may reach another device: no remote copies, remote signals or barrier semaphores. Data moves between devices by JAX's collectives and lax.ppermute only.
A program may use at most 64 MiB of HBM per device.

```python
import math
import jax
import jax.numpy as jnp
from jax import lax

C = 128
PAIR_CAP = 768
M = 4
KINDS = 8
LEVELS = 2
TX_TILES = 8
TILES = 128
NY = 2048
NX = 1024


def draw_counts(key, part):
    key = jax.random.fold_in(key, 11)
    base = jax.random.randint(jax.random.fold_in(key, 1), (TILES, TILES), PAIR_CAP // 8, PAIR_CAP // 2 + 1)
    phase = jax.random.randint(jax.random.fold_in(key, 2), (), 0, 4)
    dest = lax.broadcasted_iota(jnp.int32, (TILES, TILES), 1)
    return jnp.where(dest % 4 == phase, PAIR_CAP, base).astype(jnp.int32)


def plant(entries, rng, low, largest):
    longest = entries.shape.index(max(entries.shape))
    spots = []
    for shift in (0, 1):
        where = [jax.random.randint(jax.random.fold_in(rng, axis), (), 0, length) for axis, length in enumerate(entries.shape)]
        where[longest] = (where[longest] + shift) % entries.shape[longest]
        spots.append(tuple(where))
    return entries.at[spots[0]].set(low).at[spots[1]].set(largest)


def block_levels(rng, shape, pieces, low, largest):
    factor_of = 1.0
    for axis_at, parts in pieces:
        heights = jax.random.uniform(jax.random.fold_in(jax.random.fold_in(rng, 6), axis_at), (parts,), jnp.float32, low / len(pieces), largest / len(pieces))
        factor_of = factor_of * jnp.repeat(jnp.exp(heights), shape[axis_at] // parts).reshape((-1,) + (1,) * (len(shape) - 1 - axis_at))
    return factor_of


def noise(rng, extent, deviation, bound, pieces=(), held_as=jnp.bfloat16):
    entries = jax.random.normal(rng, extent, jnp.float32) * deviation
    if len(pieces) > 0:
        entries = block_levels(rng, extent, pieces, -0.22, 0.18) * entries
    return jnp.clip(entries, min=-bound, max=bound).astype(held_as)


def setup_inputs(seed: int = 0) -> dict:
    key_list = jax.random.split(jax.random.key(seed), 10)
    residual = noise(key_list[0], (TILES, M, TILES, PAIR_CAP), 1.0, 6.0, ((0, 128),), jnp.float32)
    counts = draw_counts(jax.random.fold_in(key_list[9], 71), 0)
    offsets = plant(jax.random.randint(key_list[2], (TILES, 2, TILES, PAIR_CAP), 2, C - 5), jax.random.fold_in(key_list[2], 1), 2, (C - 5) - 1).astype(jnp.int32)
    positions = jnp.clip(1.0 * jax.random.uniform(key_list[3], (TILES, 2, TILES, PAIR_CAP), jnp.float32) ** block_levels(key_list[3], (TILES, 2, TILES, PAIR_CAP), ((0, 128),), -0.2, 0.2), 0.0, 1.0)
    coef_fine = noise(key_list[4], (M, NY, NX), 0.05, 0.4, ((1, 16), (2, 8)), jnp.float32)
    coef_coarse = noise(key_list[5], (M, NY // 2, NX // 2), 0.05, 0.4, ((1, 16), (2, 8)), jnp.float32)
    kappa_map = plant(jax.random.randint(key_list[6], (NY, NX), 0, KINDS), jax.random.fold_in(key_list[6], 1), 0, KINDS - 1).astype(jnp.int32)
    kappa_table = jnp.clip(jnp.exp(jax.random.uniform(key_list[7], (LEVELS, KINDS), jnp.float32, math.log(0.05), math.log(3.0))), 0.05, 3.0)
    level_weight = jnp.clip(jnp.exp(jax.random.uniform(key_list[8], (LEVELS,), jnp.float32, math.log(0.5), math.log(2.0))), 0.5, 2.0)
    return {"residual": residual, "counts": counts, "offsets": offsets, "positions": positions, "coef_fine": coef_fine, "coef_coarse": coef_coarse, "kappa_map": kappa_map, "kappa_table": kappa_table, "level_weight": level_weight}


def spline(t):
    s = 1.0 - t
    return (s * s * s / 6.0, (3.0 * t * t * t - 6.0 * t * t + 4.0) / 6.0,
            (-3.0 * t * t * t + 3.0 * t * t + 3.0 * t + 1.0) / 6.0, t * t * t / 6.0)


def coarse_place(cells, fracs):
    return cells // 2, ((cells % 2).astype(fracs.dtype) + fracs) * 0.5


def tile_terms(values, cells, fracs, side):
    weight_y = spline(fracs[0])
    weight_x = spline(fracs[1])
    table = jnp.zeros((side * side, values.shape[1]), jnp.float32)
    for a in range(4):
        left = (values * weight_y[a][:, None]).astype(jnp.bfloat16)
        left = lax.optimization_barrier(left).astype(jnp.float32)
        row = cells[0] - 1 + a
        for b in range(4):
            right = weight_x[b].astype(jnp.bfloat16)
            right = lax.optimization_barrier(right).astype(jnp.float32)
            index = row * side + cells[1] - 1 + b
            table = table.at[index].add(left * right[:, None])
    return table.T.reshape(values.shape[1], side, side)


def neighbours(field):
    padded = jnp.pad(field, ((0, 0), (1, 1), (1, 1)))
    return padded[:, 2:, 1:-1] + padded[:, :-2, 1:-1] + padded[:, 1:-1, 2:] + padded[:, 1:-1, :-2]


def precision_apply(field, diag):
    first = diag * field - neighbours(field)
    return diag * first - neighbours(first)


def reference(residual, counts, offsets, positions, coef_fine, coef_coarse, kappa_map, kappa_table, level_weight):
    slots = jnp.arange(PAIR_CAP, dtype=jnp.int32)
    live = slots[None, None, None, :] < counts[:, None, :, None]
    masked = jnp.where(live, residual, 0.0)
    half = C // 2

    def one_tile(dest, grids):
        fine_grid, coarse_grid = grids
        dest = dest.astype(jnp.int32)
        values = lax.dynamic_index_in_dim(masked, dest, 2, keepdims=False)
        values = jnp.transpose(values, (0, 2, 1)).reshape(TILES * PAIR_CAP, M)
        cells = lax.dynamic_index_in_dim(offsets, dest, 0, keepdims=False)
        cells = cells.reshape(2, TILES * PAIR_CAP)
        fracs = lax.dynamic_index_in_dim(positions, dest, 0, keepdims=False)
        fracs = fracs.reshape(2, TILES * PAIR_CAP)
        fine_part = tile_terms(values, cells, fracs, C)
        coarse_cells, coarse_fracs = coarse_place(cells, fracs)
        coarse_part = tile_terms(values, coarse_cells, coarse_fracs, half)
        tile_row = (dest // TX_TILES).astype(jnp.int32)
        tile_col = (dest % TX_TILES).astype(jnp.int32)
        anchor = jnp.zeros((), jnp.int32)
        fine_grid = lax.dynamic_update_slice(fine_grid, fine_part, (anchor, tile_row * C, tile_col * C))
        coarse_grid = lax.dynamic_update_slice(coarse_grid, coarse_part, (anchor, tile_row * half, tile_col * half))
        return fine_grid, coarse_grid

    start = (jnp.zeros((M, NY, NX), jnp.float32), jnp.zeros((M, NY // 2, NX // 2), jnp.float32))
    fine_proj, coarse_proj = lax.fori_loop(0, TILES, one_tile, start)
    diag_fine = 4.0 + kappa_table[0][kappa_map]
    diag_coarse = 4.0 + kappa_table[1][kappa_map[::2, ::2]]
    fine_grad = level_weight[0] * fine_proj - precision_apply(coef_fine, diag_fine)
    coarse_grad = level_weight[1] * coarse_proj - precision_apply(coef_coarse, diag_coarse)
    return fine_grad, coarse_grad
```

```python
import functools

import jax
import jax.numpy as jnp
from jax import lax
from jax.experimental import pallas as pl
from jax.experimental.pallas import tpu as pltpu
from jax.sharding import PartitionSpec as P

BF = jnp.bfloat16
F = jnp.float32
VMEM_LIMIT = 48 * 1024 * 1024
AXES = ("ty", "tx")


def struct(*shape):
    return jax.ShapeDtypeStruct(shape, F)


def iota(shape, dim):
    return lax.broadcasted_iota(jnp.int32, shape, dim)


def mm(a, b, dims=((1,), (0,))):
    return lax.dot_general(a, b, (dims, ((), ())), preferred_element_type=F)


def split3(a):
    hi = a.astype(BF)
    a = a - hi.astype(F)
    mid = a.astype(BF)
    lo = (a - mid.astype(F)).astype(BF)
    return hi, mid, lo


def params():
    return pltpu.CompilerParams(vmem_limit_bytes=VMEM_LIMIT)


def pack_kernel(block, counts_ref, res_ref, out_ref):
    base = pl.program_id(0) * block
    chunks = res_ref.shape[2] // 128
    own = iota((block, 128), 0) + base == iota((block, 128), 1)
    live = jnp.sum(jnp.where(own, counts_ref[...], 0).astype(F), axis=1, keepdims=True).astype(jnp.int32)
    for d in range(0, block, 8):
        for kc in range(chunks):
            slot = iota((8, 128), 1) + 128 * kc
            keep = slot < live[d:d + 8]
            for m in range(4):
                row = (d * chunks + kc) * 4 + m
                value = jnp.where(keep, res_ref[m, d:d + 8, 128 * kc:128 * kc + 128], 0.0)
                out_ref[pl.ds(row, 8, stride=4 * chunks), :] = value


def pack(counts, residual):
    channels, tiles, slots = residual.shape
    block = 32
    rows = 4 * (slots // 128)
    return pl.pallas_call(
        functools.partial(pack_kernel, block),
        grid=(tiles // block,),
        in_specs=[
            pl.BlockSpec((1, tiles), lambda i: (0, 0)),
            pl.BlockSpec((channels, block, slots), lambda i: (0, i, 0)),
        ],
        out_specs=pl.BlockSpec((block * rows, 128), lambda i: (i, 0)),
        out_shape=struct(tiles * rows, 128),
        compiler_params=params(),
        name="pack_rows",
    )(counts, residual)


def classes_to_diag(kinds, table_ref, level):
    total = jnp.zeros(kinds.shape, F)
    for k in range(table_ref.shape[1]):
        total = jnp.where(kinds == k, table_ref[level, k], total)
    return 4.0 + total


def columns_kernel(table_ref, cf_ref, cc_ref, km_ref, left_ref, right_ref, df_ref, dc_ref, square):
    left_ref[...] = jnp.zeros_like(left_ref)
    right_ref[...] = jnp.zeros_like(right_ref)
    square[...] = jnp.zeros_like(square)
    df = classes_to_diag(km_ref[...], table_ref, 0)
    df_ref[...] = df
    even = km_ref[pl.ds(0, 64, stride=2), :].astype(F).astype(BF)
    pick = jnp.where(iota((128, 128), 0) == 2 * iota((128, 128), 1), 1.0, 0.0).astype(BF)
    dc = classes_to_diag(mm(even, pick).astype(jnp.int32), table_ref, 1)
    dc = jnp.where(iota((64, 128), 1) < 64, dc, 0.0)
    dc_ref[...] = dc

    def send(row, turned, size, width):
        left_ref[pl.ds(row, width), :] = turned[0:width]
        right_ref[pl.ds(row, width), :] = turned[size - width:size]

    for m in range(4):
        send(2 * m, cf_ref[m].T, 128, 2)
        square[0:64, 0:64] = cc_ref[m]
        send(8 + 2 * m, square[...].T, 64, 2)
    send(16, df.T, 128, 1)
    square[0:64, :] = dc
    send(17, square[...].T, 64, 1)


def rows_kernel(cf_ref, cc_ref, df_ref, dc_ref, fl_ref, fr_ref, up_ref, down_ref, cs_ref, cm_ref, ds_ref, dm_ref, square):
    up_ref[...] = jnp.zeros_like(up_ref)
    down_ref[...] = jnp.zeros_like(down_ref)

    def sides(row, first, width):
        square[...] = jnp.zeros_like(square)
        square[first:first + width, :] = fr_ref[row:row + width, :]
        square[128 - width:128, :] = fl_ref[row:row + width, :]
        return square[...].T

    def send(row, lane, field, size, width):
        lanes = pl.ds(lane, 128)
        up_ref[pl.ds(row, width), lanes] = field[0:width]
        down_ref[pl.ds(row, width), lanes] = field[size - width:size]

    for m in range(4):
        side = sides(2 * m, 0, 2)
        cs_ref[m] = side
        send(2 * m, 0, cf_ref[m], 128, 2)
        send(2 * m, 128, side, 128, 2)
        cm_ref[m] = sides(8 + 2 * m, 64, 2)[0:64]
        cm_ref[m, :, 0:64] = cc_ref[m]
        send(8 + 2 * m, 0, cm_ref[m], 64, 2)
    side = sides(16, 0, 1)
    ds_ref[...] = side
    send(16, 0, df_ref[...], 128, 1)
    send(16, 128, side, 128, 1)
    dm_ref[...] = dc_ref[...] + sides(17, 64, 1)[0:64]
    send(17, 0, dm_ref[...], 64, 1)


def stencil_kernel(cf_ref, cs_ref, cm_ref, df_ref, ds_ref, dm_ref, fu_ref, fd_ref, bf_ref, bc_ref, vf, wf, vc, wc):
    def apply(field, diag):
        rows, lanes = field.shape
        near = pltpu.roll(field, 1, 0) + pltpu.roll(field, rows - 1, 0)
        near = near + (pltpu.roll(field, 1, 1) + pltpu.roll(field, lanes - 1, 1))
        return diag * field - near

    def twice(field, diag):
        first = jnp.where(diag > 0.0, apply(field, diag), 0.0)
        return apply(first, diag)

    def edges(scratch, size, row, width, lanes):
        last = scratch.shape[0]
        scratch[size:last, :] = jnp.zeros((last - size, lanes), F)
        scratch[size:size + width, :] = fd_ref[row:row + width, 0:lanes]
        scratch[last - width:last, :] = fu_ref[row:row + width, 0:lanes]

    wf[0:128, 0:128] = df_ref[...]
    wf[0:128, 128:256] = ds_ref[...]
    edges(wf, 128, 16, 1, 256)
    wc[0:64, :] = dm_ref[...]
    edges(wc, 64, 17, 1, 128)
    for m in range(4):
        vf[0:128, 0:128] = cf_ref[m]
        vf[0:128, 128:256] = cs_ref[m]
        edges(vf, 128, 2 * m, 2, 256)
        bf_ref[m] = twice(vf[...], wf[...])[0:128, 0:128]
        vc[0:64, :] = cm_ref[m]
        edges(vc, 64, 8 + 2 * m, 2, 128)
        bc_ref[m] = twice(vc[...], wc[...])[0:64, 0:64]


def neighbours(axis):
    count = lax.axis_size(axis)
    up = [(i, i + 1) for i in range(count - 1)]
    return up, [(j, i) for i, j in up]


def precision(coef_fine, coef_coarse, kappa_map, kappa_table):
    smem = pl.BlockSpec(memory_space=pltpu.SMEM)
    vmem = pl.BlockSpec(memory_space=pltpu.VMEM)
    square = pltpu.VMEM((128, 128), F)
    to_left, to_right, df, dc = pl.pallas_call(
        columns_kernel,
        in_specs=[smem] + [vmem] * 3,
        out_shape=[struct(24, 128), struct(24, 128), struct(128, 128), struct(64, 128)],
        scratch_shapes=[square],
        compiler_params=params(),
        name="edge_columns",
    )(kappa_table, coef_fine, coef_coarse, kappa_map)
    onward, back = neighbours("tx")
    from_left = lax.ppermute(to_right, "tx", onward)
    from_right = lax.ppermute(to_left, "tx", back)
    to_up, to_down, side, coarse, dside, dcoarse = pl.pallas_call(
        rows_kernel,
        out_shape=[struct(24, 256), struct(24, 256), struct(4, 128, 128), struct(4, 64, 128), struct(128, 128), struct(64, 128)],
        scratch_shapes=[square],
        compiler_params=params(),
        name="edge_rows",
    )(coef_fine, coef_coarse, df, dc, from_left, from_right)
    onward, back = neighbours("ty")
    from_up = lax.ppermute(to_down, "ty", onward)
    from_down = lax.ppermute(to_up, "ty", back)
    return pl.pallas_call(
        stencil_kernel,
        out_shape=[struct(4, 128, 128), struct(4, 64, 64)],
        scratch_shapes=[pltpu.VMEM((136, 256), F), pltpu.VMEM((136, 256), F), pltpu.VMEM((72, 128), F), pltpu.VMEM((72, 128), F)],
        compiler_params=params(),
        name="stencil_twice",
    )(coef_fine, side, coarse, df, dside, dcoarse, from_up, from_down)


def spline(t):
    s = 1.0 - t
    return (
        s * s * s / 6.0,
        (3.0 * t * t * t - 6.0 * t * t + 4.0) / 6.0,
        (-3.0 * t * t * t + 3.0 * t * t + 3.0 * t + 1.0) / 6.0,
        t * t * t / 6.0,
    )


def rotate(weights, start):
    odd = (start & 1) == 1
    weights = [jnp.where(odd, weights[(r - 1) % 4], weights[r]) for r in range(4)]
    two = (start & 2) == 2
    return [jnp.where(two, weights[(r - 2) % 4], weights[r]) for r in range(4)]


def project_kernel(steps, group, slots, lw_ref, v_ref, off_ref, pos_ref, bf_ref, bc_ref, fine_ref, coarse_ref, rows, acc):
    step = pl.program_id(0)

    @pl.when(step == 0)
    def _():
        acc[...] = jnp.zeros_like(acc)

    chunks = slots // 128
    sy = off_ref[0] - 2
    sx = off_ref[1] - 2
    upper = sy >= 61
    sy = jnp.where(upper, sy - 61, sy)
    by = sy & 3
    bx = sx & 3
    qy = sy >> 2
    qx = (sx >> 2) + jnp.where(upper, 32, 0)
    wy = rotate(spline(pos_ref[0]), by)
    wx = rotate(spline(pos_ref[1]), bx)
    for r in range(4):
        rows[r] = (qy + jnp.where(by > r, 1, 0)).astype(F)
        rows[4 + r] = (qx + jnp.where(bx > r, 1, 0)).astype(F)
        rows[8 + r] = wx[r]
    for m in range(4):
        v = jnp.concatenate([v_ref[pl.ds(4 * kc + m, group, stride=4 * chunks), :] for kc in range(chunks)], 1)
        for r in range(4):
            rows[12 + 4 * m + r] = v * wy[r]
    i16 = iota((16, slots), 0).astype(F).astype(BF)
    i64 = iota((64, slots), 0).astype(F).astype(BF)
    zero = jnp.zeros((), BF)

    def spread(i, s, n):
        row = jnp.broadcast_to(rows[i, pl.ds(s, 1), :], (16, slots)).astype(BF)
        return jnp.broadcast_to(row[None], (n // 16, 16, slots)).reshape(n, slots)

    for s in range(group):
        left = [None] * 16
        for r in range(4):
            here = i16 == spread(r, s, 16)
            for m in range(4):
                left[4 * m + r] = jnp.where(here, spread(12 + 4 * m + r, s, 16), zero)
        right = [jnp.where(i64 == spread(4 + r, s, 64), spread(8 + r, s, 64), zero) for r in range(4)]
        acc[...] += mm(jnp.concatenate(left, 0), jnp.concatenate(right, 0), ((1,), (1,)))

    @pl.when(step == steps - 1)
    def _():
        a = iota((256, 256), 0)
        b = iota((256, 256), 1)
        place = ((b >> 7) == ((a >> 5) & 1)) & ((b & 127) == 1 + 4 * (a & 31) + (a >> 6))
        place = jnp.where(place, 1.0, 0.0).astype(BF)
        wide = sum(mm(p, place) for p in split3(acc[...]))
        ya = iota((128, 64), 0)
        yb = iota((128, 64), 1)
        row = 1 + 4 * (yb & 15) + (yb >> 4)
        lift = [jnp.where(ya == row + 61 * h, 1.0, 0.0).astype(BF) for h in range(2)]
        far = jnp.abs(iota((64, 128), 1) - 2 * iota((64, 128), 0))
        halve = jnp.where(far == 0, 0.75, jnp.where(far == 1, 0.5, jnp.where(far == 2, 0.125, 0.0))).astype(BF)
        for m in range(4):
            part = wide[m * 64:(m + 1) * 64]
            fine = sum(mm(lift[h], p) for h in range(2) for p in split3(part[:, h * 128:(h + 1) * 128]))
            fine_ref[m] = lw_ref[0] * fine - bf_ref[m]
            coarse = sum(mm(halve, p) for p in split3(fine))
            coarse = sum(mm(p, halve, ((1,), (1,))) for p in split3(coarse))
            coarse_ref[m] = lw_ref[1] * coarse - bc_ref[m]


def project(values, offsets, positions, level_weight, fine, coarse):
    tiles, slots = offsets.shape[1:]
    group = 16
    steps = tiles // group
    whole = [pl.BlockSpec((4, 128, 128), lambda i: (0, 0, 0)), pl.BlockSpec((4, 64, 64), lambda i: (0, 0, 0))]
    return pl.pallas_call(
        functools.partial(project_kernel, steps, group, slots),
        grid=(steps,),
        in_specs=[
            pl.BlockSpec(memory_space=pltpu.SMEM),
            pl.BlockSpec((group * slots // 32, 128), lambda i: (i, 0)),
            pl.BlockSpec((2, group, slots), lambda i: (0, i, 0)),
            pl.BlockSpec((2, group, slots), lambda i: (0, i, 0)),
        ] + whole,
        out_specs=whole,
        out_shape=[struct(4, 128, 128), struct(4, 64, 64)],
        scratch_shapes=[pltpu.VMEM((28, group, slots), F), pltpu.VMEM((256, 256), F)],
        compiler_params=params(),
        name="project_rows",
    )(level_weight, values, offsets, positions, fine, coarse)


def on_device(residual, counts, offsets, positions, coef_fine, coef_coarse, kappa_map, kappa_table, level_weight):
    tiles = residual.shape[2]
    packed = pack(counts, residual[0])
    packed = packed.reshape(tiles, -1, 128)
    arrived = lax.all_to_all(packed, AXES, split_axis=0, concat_axis=0, tiled=True)
    fine, coarse = precision(coef_fine, coef_coarse, kappa_map, kappa_table)
    return tuple(project(arrived.reshape(-1, 128), offsets[0], positions[0], level_weight, fine, coarse))


def solution(mesh):
    rows = P(AXES, None, None, None)
    tile = P(None, "ty", "tx")
    return jax.shard_map(
        on_device,
        mesh=mesh,
        in_specs=(rows, P(AXES, None), rows, rows, tile, tile, P("ty", "tx"), P(), P()),
        out_specs=(tile, tile),
        check_vma=False,
    )
```

```python
import functools

import jax
import jax.numpy as jnp
from jax import lax
from jax.experimental import pallas as pl
from jax.experimental.pallas import tpu as pltpu
from jax.sharding import PartitionSpec as P

BF = jnp.bfloat16
F = jnp.float32
VMEM_LIMIT = 48 * 1024 * 1024
AXES = ("ty", "tx")


def struct(*shape):
    return jax.ShapeDtypeStruct(shape, F)


def iota(shape, dim):
    return lax.broadcasted_iota(jnp.int32, shape, dim)


def mm(a, b, dims=((1,), (0,))):
    return lax.dot_general(a, b, (dims, ((), ())), preferred_element_type=F)


def split3(a):
    hi = a.astype(BF)
    a = a - hi.astype(F)
    mid = a.astype(BF)
    lo = (a - mid.astype(F)).astype(BF)
    return hi, mid, lo


def params():
    return pltpu.CompilerParams(vmem_limit_bytes=VMEM_LIMIT)


def pack_kernel(block, counts_ref, res_ref, out_ref, loaded, built, sems, out_sems):
    tiles, slots = res_ref.shape[1:]
    parts = tiles // block
    chunks = slots // 128
    rows = 4 * chunks * block
    loads = [
        pltpu.make_async_copy(res_ref.at[:, pl.ds(i * block, block), :], loaded.at[i], sems.at[i]) for i in range(parts)
    ]
    for load in loads:
        load.start()
    stores = []
    for i in range(parts):
        loads[i].wait()
        for d in range(0, block, 8):
            live = jnp.zeros((8, 128), jnp.int32)
            for j in range(8):
                live = jnp.where(iota((8, 128), 0) == j, counts_ref[0, i * block + d + j], live)
            for kc in range(chunks):
                keep = iota((8, 128), 1) + 128 * kc < live
                for m in range(4):
                    row = (d * chunks + kc) * 4 + m
                    value = jnp.where(keep, loaded[i, m, d:d + 8, 128 * kc:128 * kc + 128], 0.0)
                    built[i, pl.ds(row, 8, stride=4 * chunks), :] = value
        store = pltpu.make_async_copy(built.at[i], out_ref.at[pl.ds(i * rows, rows), :], out_sems.at[i])
        store.start()
        stores.append(store)
    for store in stores:
        store.wait()


def pack(counts, residual):
    channels, tiles, slots = residual.shape
    block = 16
    parts = tiles // block
    rows = 4 * (slots // 128)
    return pl.pallas_call(
        functools.partial(pack_kernel, block),
        in_specs=[pl.BlockSpec(memory_space=pltpu.SMEM), pl.BlockSpec(memory_space=pltpu.HBM)],
        out_specs=pl.BlockSpec(memory_space=pl.ANY),
        out_shape=struct(tiles * rows, 128),
        scratch_shapes=[
            pltpu.VMEM((parts, channels, block, slots), F),
            pltpu.VMEM((parts, block * rows, 128), F),
            pltpu.SemaphoreType.DMA((parts,)),
            pltpu.SemaphoreType.DMA((parts,)),
        ],
        compiler_params=pltpu.CompilerParams(vmem_limit_bytes=62 * 1024 * 1024),
        name="pack_rows",
    )(counts, residual)


def classes_to_diag(kinds, table_ref, level):
    total = jnp.zeros(kinds.shape, F)
    for k in range(table_ref.shape[1]):
        total = jnp.where(kinds == k, table_ref[level, k], total)
    return 4.0 + total


def columns_kernel(table_ref, cf_ref, cc_ref, km_ref, left_ref, right_ref, df_ref, dc_ref, square):
    left_ref[...] = jnp.zeros_like(left_ref)
    right_ref[...] = jnp.zeros_like(right_ref)
    square[...] = jnp.zeros_like(square)
    df = classes_to_diag(km_ref[...], table_ref, 0)
    df_ref[...] = df
    even = km_ref[pl.ds(0, 64, stride=2), :].astype(F).astype(BF)
    pick = jnp.where(iota((128, 128), 0) == 2 * iota((128, 128), 1), 1.0, 0.0).astype(BF)
    dc = classes_to_diag(mm(even, pick).astype(jnp.int32), table_ref, 1)
    dc = jnp.where(iota((64, 128), 1) < 64, dc, 0.0)
    dc_ref[...] = dc

    def send(row, turned, size, width):
        left_ref[pl.ds(row, width), :] = turned[0:width]
        right_ref[pl.ds(row, width), :] = turned[size - width:size]

    for m in range(4):
        send(2 * m, cf_ref[m].T, 128, 2)
        square[0:64, 0:64] = cc_ref[m]
        send(8 + 2 * m, square[...].T, 64, 2)
    send(16, df.T, 128, 1)
    square[0:64, :] = dc
    send(17, square[...].T, 64, 1)


def rows_kernel(cf_ref, cc_ref, df_ref, dc_ref, fl_ref, fr_ref, at_ref, up_ref, down_ref, cs_ref, cm_ref, ds_ref, dm_ref, square):
    up_ref[...] = jnp.zeros_like(up_ref)
    down_ref[...] = jnp.zeros_like(down_ref)

    def sides(row, first, width):
        square[...] = jnp.zeros_like(square)
        square[first:first + width, :] = fr_ref[row:row + width, :]
        square[128 - width:128, :] = fl_ref[row:row + width, :]
        return square[...].T

    def send(row, lane, field, size, width):
        lanes = pl.ds(lane, 128)
        up_ref[pl.ds(row, width), lanes] = field[0:width]
        down_ref[pl.ds(row, width), lanes] = field[size - width:size]

    for m in range(4):
        side = sides(2 * m, 0, 2)
        cs_ref[m] = side
        send(2 * m, 0, cf_ref[m], 128, 2)
        send(2 * m, 128, side, 128, 2)
        cm_ref[m] = sides(8 + 2 * m, 64, 2)[0:64]
        cm_ref[m, :, 0:64] = cc_ref[m]
        send(8 + 2 * m, 0, cm_ref[m], 64, 2)
    side = sides(16, 0, 1)
    ds_ref[...] = side
    send(16, 0, df_ref[...], 128, 1)
    send(16, 128, side, 128, 1)
    dm_ref[...] = dc_ref[...] + sides(17, 64, 1)[0:64]
    send(17, 0, dm_ref[...], 64, 1)


def finish_kernel(lw_ref, acc, cf_ref, cs_ref, cm_ref, df_ref, ds_ref, dm_ref, fu_ref, fd_ref, fine_ref, coarse_ref, vf, wf, vc, wc, tall, low):
    def apply(field, diag):
        rows, lanes = field.shape
        near = pltpu.roll(field, 1, 0) + pltpu.roll(field, rows - 1, 0)
        near = near + (pltpu.roll(field, 1, 1) + pltpu.roll(field, lanes - 1, 1))
        return diag * field - near

    def twice(field, diag):
        first = jnp.where(diag > 0.0, apply(field, diag), 0.0)
        return apply(first, diag)

    def rim(scratch, size, row, width, lanes):
        last = scratch.shape[0]
        scratch[size:last, :] = jnp.zeros((last - size, lanes), F)
        scratch[size:size + width, :] = fd_ref[row:row + width, 0:lanes]
        scratch[last - width:last, :] = fu_ref[row:row + width, 0:lanes]

    wf[0:128, 0:128] = df_ref[...]
    wf[0:128, 128:256] = ds_ref[...]
    rim(wf, 128, 16, 1, 256)
    wc[0:64, :] = dm_ref[...]
    rim(wc, 64, 17, 1, 128)
    for m in range(4):
        vf[0:128, 0:128] = cf_ref[m]
        vf[0:128, 128:256] = cs_ref[m]
        rim(vf, 128, 2 * m, 2, 256)
        fine_ref[m] = twice(vf[...], wf[...])[0:128, 0:128]
        vc[0:64, :] = cm_ref[m]
        rim(vc, 64, 8 + 2 * m, 2, 128)
        coarse_ref[m] = twice(vc[...], wc[...])[0:64, 0:64]

    a = iota((256, 256), 0)
    b = iota((256, 256), 1)
    place = ((b >> 7) == ((a >> 5) & 1)) & ((b & 127) == 1 + 4 * (a & 31) + (a >> 6))
    place = jnp.where(place, 1.0, 0.0).astype(BF)
    wide = sum(mm(p, place) for p in split3(acc[...]))
    far = jnp.abs(iota((128, 128), 0) - 2 * iota((128, 128), 1))
    halve = jnp.where(far == 0, 0.75, jnp.where(far == 1, 0.5, jnp.where(far == 2, 0.125, 0.0))).astype(BF)
    for m in range(4):
        tall[m, 0:16, :] = jnp.zeros((16, 128), F)
        tall[m, 72:144, :] = jnp.zeros((72, 128), F)
        for h in range(2):
            for r in range(4):
                at = m * 64 + r * 16
                spots = pl.ds(9 + 61 * h + r, 16, stride=4)
                part = wide[at:at + 16, h * 128:(h + 1) * 128]
                tall[m, spots, :] = part if h == 0 else part + tall[m, spots, :]
        fine_ref[m] = lw_ref[0] * tall[m, 8:136, :] - fine_ref[m]
        every = [tall[m, pl.ds(8 + k, 64, stride=2), :] for k in range(-2, 3)]
        low[m * 64:(m + 1) * 64, :] = 0.75 * every[2] + 0.5 * (every[1] + every[3]) + 0.125 * (every[0] + every[4])
    coarse = sum(mm(p, halve) for p in split3(low[...]))
    for m in range(4):
        coarse_ref[m] = lw_ref[1] * coarse[m * 64:(m + 1) * 64, 0:64] - coarse_ref[m]


def neighbours(axis):
    count = lax.axis_size(axis)
    up = [(i, i + 1) for i in range(count - 1)]
    return up, [(j, i) for i, j in up]


def edges(coef_fine, coef_coarse, kappa_map, kappa_table, at):
    smem = pl.BlockSpec(memory_space=pltpu.SMEM)
    vmem = pl.BlockSpec(memory_space=pltpu.VMEM)
    square = pltpu.VMEM((128, 128), F)
    to_left, to_right, df, dc = pl.pallas_call(
        columns_kernel,
        in_specs=[smem] + [vmem] * 3,
        out_shape=[struct(24, 128), struct(24, 128), struct(128, 128), struct(64, 128)],
        scratch_shapes=[square],
        compiler_params=params(),
        name="edge_columns",
    )(kappa_table, coef_fine, coef_coarse, kappa_map)
    onward, back = neighbours("tx")
    from_left = lax.ppermute(to_right, "tx", onward)
    from_right = lax.ppermute(to_left, "tx", back)
    to_up, to_down, side, coarse, dside, dcoarse = pl.pallas_call(
        rows_kernel,
        in_specs=[vmem] * 6 + [pl.BlockSpec(memory_space=pl.ANY)],
        out_shape=[struct(24, 256), struct(24, 256), struct(4, 128, 128), struct(4, 64, 128), struct(128, 128), struct(64, 128)],
        scratch_shapes=[square],
        compiler_params=params(),
        name="edge_rows",
    )(coef_fine, coef_coarse, df, dc, from_left, from_right, at)
    onward, back = neighbours("ty")
    from_up = lax.ppermute(to_down, "ty", onward)
    from_down = lax.ppermute(to_up, "ty", back)
    return coef_fine, side, coarse, df, dside, dcoarse, from_up, from_down


def finish(level_weight, total, fields):
    vmem = pl.BlockSpec(memory_space=pltpu.VMEM)
    return pl.pallas_call(
        finish_kernel,
        in_specs=[pl.BlockSpec(memory_space=pltpu.SMEM)] + [vmem] * (1 + len(fields)),
        out_shape=[struct(4, 128, 128), struct(4, 64, 64)],
        scratch_shapes=[
            pltpu.VMEM((136, 256), F),
            pltpu.VMEM((136, 256), F),
            pltpu.VMEM((72, 128), F),
            pltpu.VMEM((72, 128), F),
            pltpu.VMEM((4, 144, 128), F),
            pltpu.VMEM((256, 128), F),
        ],
        compiler_params=params(),
        name="finish_tiles",
    )(level_weight, total, *fields)


def spline(t):
    s = 1.0 - t
    return (
        s * s * s / 6.0,
        (3.0 * t * t * t - 6.0 * t * t + 4.0) / 6.0,
        (-3.0 * t * t * t + 3.0 * t * t + 3.0 * t + 1.0) / 6.0,
        t * t * t / 6.0,
    )


def rotate(weights, start):
    odd = (start & 1) == 1
    weights = [jnp.where(odd, weights[(r - 1) % 4], weights[r]) for r in range(4)]
    two = (start & 2) == 2
    return [jnp.where(two, weights[(r - 2) % 4], weights[r]) for r in range(4)]


def place_kernel(off_ref, pos_ref, out_ref):
    sy = off_ref[0] - 2
    sx = off_ref[1] - 2
    upper = sy >= 61
    sy = jnp.where(upper, sy - 61, sy)
    by = sy & 3
    bx = sx & 3
    qy = sy >> 2
    qx = (sx >> 2) + jnp.where(upper, 32, 0)
    wy = rotate(spline(pos_ref[0]), by)
    wx = rotate(spline(pos_ref[1]), bx)
    for r in range(4):
        out_ref[r] = (qy + jnp.where(by > r, 1, 0)).astype(F)
        out_ref[4 + r] = (qx + jnp.where(bx > r, 1, 0)).astype(F)
        out_ref[8 + r] = wx[r]
        out_ref[12 + r] = wy[r]


def places(offsets, positions):
    tiles, slots = offsets.shape[1:]
    group = 16
    points = pl.BlockSpec((2, group, slots), lambda i: (0, i, 0))
    return pl.pallas_call(
        place_kernel,
        grid=(tiles // group,),
        in_specs=[points, points],
        out_specs=pl.BlockSpec((16, group, slots), lambda i: (0, i, 0)),
        out_shape=struct(16, tiles, slots),
        compiler_params=params(),
        name="place_rows",
    )(offsets, positions)


def project_kernel(group, slots, v_ref, at_ref, acc, values):
    @pl.when(pl.program_id(0) == 0)
    def _():
        acc[...] = jnp.zeros_like(acc)

    chunks = slots // 128
    for m in range(4):
        v = jnp.concatenate([v_ref[pl.ds(4 * kc + m, group, stride=4 * chunks), :] for kc in range(chunks)], 1)
        for r in range(4):
            values[4 * m + r] = v * at_ref[12 + r]
    i16 = iota((16, slots), 0).astype(F).astype(BF)
    i64 = iota((64, slots), 0).astype(F).astype(BF)
    zero = jnp.zeros((), BF)

    def spread(ref, i, s, n):
        row = jnp.broadcast_to(ref[i, pl.ds(s, 1), :], (16, slots)).astype(BF)
        return jnp.broadcast_to(row[None], (n // 16, 16, slots)).reshape(n, slots)

    def build(s):
        left = [None] * 16
        for r in range(4):
            here = i16 == spread(at_ref, r, s, 16)
            for m in range(4):
                left[4 * m + r] = jnp.where(here, spread(values, 4 * m + r, s, 16), zero)
        right = [jnp.where(i64 == spread(at_ref, 4 + r, s, 64), spread(at_ref, 8 + r, s, 64), zero) for r in range(4)]
        return jnp.concatenate(left, 0), jnp.concatenate(right, 0)

    for s in range(group):
        left, right = build(s)
        acc[...] += mm(left, right, ((1,), (1,)))


def project(values, at):
    tiles, slots = at.shape[1:]
    group = 32
    return pl.pallas_call(
        functools.partial(project_kernel, group, slots),
        grid=(tiles // group,),
        in_specs=[
            pl.BlockSpec((group * slots // 32, 128), lambda i: (i, 0)),
            pl.BlockSpec((16, group, slots), lambda i: (0, i, 0)),
        ],
        out_specs=pl.BlockSpec((256, 256), lambda i: (0, 0)),
        out_shape=struct(256, 256),
        scratch_shapes=[pltpu.VMEM((16, group, slots), F)],
        compiler_params=params(),
        name="project_rows",
    )(values, at)


def on_device(residual, counts, offsets, positions, coef_fine, coef_coarse, kappa_map, kappa_table, level_weight):
    tiles = residual.shape[2]
    packed = pack(counts, residual[0]).reshape(tiles, -1, 4, 128)
    values = lax.all_to_all(packed, AXES, split_axis=0, concat_axis=0, tiled=True).reshape(-1, 128)
    at = places(offsets[0], positions[0])
    fields = edges(coef_fine, coef_coarse, kappa_map, kappa_table, at)
    return tuple(finish(level_weight, project(values, at), fields))


def solution(mesh):
    rows = P(AXES, None, None, None)
    tile = P(None, "ty", "tx")
    return jax.shard_map(
        on_device,
        mesh=mesh,
        in_specs=(rows, P(AXES, None), rows, rows, tile, tile, P("ty", "tx"), P(), P()),
        out_specs=(tile, tile),
        check_vma=False,
    )
```

```python
import functools

import jax
import jax.numpy as jnp
from jax import lax
from jax.experimental import pallas as pl
from jax.experimental.pallas import tpu as pltpu
from jax.sharding import PartitionSpec as P

BF = jnp.bfloat16
F = jnp.float32
VMEM_LIMIT = 48 * 1024 * 1024
AXES = ("ty", "tx")


def struct(*shape):
    return jax.ShapeDtypeStruct(shape, F)


def iota(shape, dim):
    return lax.broadcasted_iota(jnp.int32, shape, dim)


def mm(a, b, dims=((1,), (0,))):
    return lax.dot_general(a, b, (dims, ((), ())), preferred_element_type=F)


def split3(a):
    hi = a.astype(BF)
    a = a - hi.astype(F)
    mid = a.astype(BF)
    lo = (a - mid.astype(F)).astype(BF)
    return hi, mid, lo


def params():
    return pltpu.CompilerParams(vmem_limit_bytes=VMEM_LIMIT)


def pack_kernel(block, counts_ref, res_ref, out_ref, counts, loaded, built, sems, out_sems, count_sem):
    tiles, slots = res_ref.shape[1:]
    parts = tiles // block
    chunks = slots // 128
    rows = 4 * chunks * block
    take = pltpu.make_async_copy(counts_ref, counts, count_sem)
    take.start()
    loads = [
        pltpu.make_async_copy(res_ref.at[:, pl.ds(i * block, block), :], loaded.at[i], sems.at[i]) for i in range(parts)
    ]
    for load in loads:
        load.start()
    take.wait()
    stores = []
    for i in range(parts):
        loads[i].wait()
        for d in range(0, block, 8):
            live = jnp.zeros((8, 128), jnp.int32)
            for j in range(8):
                live = jnp.where(iota((8, 128), 0) == j, counts[0, i * block + d + j], live)
            for kc in range(chunks):
                keep = iota((8, 128), 1) + 128 * kc < live
                for m in range(4):
                    row = (d * chunks + kc) * 4 + m
                    value = jnp.where(keep, loaded[i, m, d:d + 8, 128 * kc:128 * kc + 128], 0.0)
                    built[i, pl.ds(row, 8, stride=4 * chunks), :] = value
        store = pltpu.make_async_copy(built.at[i], out_ref.at[pl.ds(i * rows, rows), :], out_sems.at[i])
        store.start()
        stores.append(store)
    for store in stores:
        store.wait()


def pack(counts, residual):
    channels, tiles, slots = residual.shape
    block = 32
    parts = tiles // block
    rows = 4 * (slots // 128)
    return pl.pallas_call(
        functools.partial(pack_kernel, block),
        in_specs=[pl.BlockSpec(memory_space=pltpu.HBM)] * 2,
        out_specs=pl.BlockSpec(memory_space=pl.ANY),
        out_shape=struct(tiles * rows, 128),
        scratch_shapes=[
            pltpu.SMEM((1, tiles), jnp.int32),
            pltpu.VMEM((parts, channels, block, slots), F),
            pltpu.VMEM((parts, block * rows, 128), F),
            pltpu.SemaphoreType.DMA((parts,)),
            pltpu.SemaphoreType.DMA((parts,)),
            pltpu.SemaphoreType.DMA,
        ],
        compiler_params=pltpu.CompilerParams(vmem_limit_bytes=62 * 1024 * 1024),
        name="pack_rows",
    )(counts, residual)


def classes_to_diag(kinds, table_ref, level):
    total = jnp.zeros(kinds.shape, F)
    for k in range(table_ref.shape[1]):
        total = jnp.where(kinds == k, table_ref[level, k], total)
    return 4.0 + total


def columns_kernel(table_ref, cf_ref, cc_ref, km_ref, left_ref, right_ref, df_ref, dc_ref, square):
    left_ref[...] = jnp.zeros_like(left_ref)
    right_ref[...] = jnp.zeros_like(right_ref)
    square[...] = jnp.zeros_like(square)
    df = classes_to_diag(km_ref[...], table_ref, 0)
    df_ref[...] = df
    even = km_ref[pl.ds(0, 64, stride=2), :].astype(F).astype(BF)
    pick = jnp.where(iota((128, 128), 0) == 2 * iota((128, 128), 1), 1.0, 0.0).astype(BF)
    dc = classes_to_diag(mm(even, pick).astype(jnp.int32), table_ref, 1)
    dc = jnp.where(iota((64, 128), 1) < 64, dc, 0.0)
    dc_ref[...] = dc

    def send(row, turned, size, width):
        left_ref[pl.ds(row, width), :] = turned[0:width]
        right_ref[pl.ds(row, width), :] = turned[size - width:size]

    for m in range(4):
        send(2 * m, cf_ref[m].T, 128, 2)
        square[0:64, 0:64] = cc_ref[m]
        send(8 + 2 * m, square[...].T, 64, 2)
    send(16, df.T, 128, 1)
    square[0:64, :] = dc
    send(17, square[...].T, 64, 1)


def rows_kernel(cf_ref, cc_ref, df_ref, dc_ref, fl_ref, fr_ref, at_ref, up_ref, down_ref, cs_ref, cm_ref, ds_ref, dm_ref, square):
    up_ref[...] = jnp.zeros_like(up_ref)
    down_ref[...] = jnp.zeros_like(down_ref)

    def sides(row, first, width):
        square[...] = jnp.zeros_like(square)
        square[first:first + width, :] = fr_ref[row:row + width, :]
        square[128 - width:128, :] = fl_ref[row:row + width, :]
        return square[...].T

    def send(row, lane, field, size, width):
        lanes = pl.ds(lane, 128)
        up_ref[pl.ds(row, width), lanes] = field[0:width]
        down_ref[pl.ds(row, width), lanes] = field[size - width:size]

    for m in range(4):
        side = sides(2 * m, 0, 2)
        cs_ref[m] = side
        send(2 * m, 0, cf_ref[m], 128, 2)
        send(2 * m, 128, side, 128, 2)
        cm_ref[m] = sides(8 + 2 * m, 64, 2)[0:64]
        cm_ref[m, :, 0:64] = cc_ref[m]
        send(8 + 2 * m, 0, cm_ref[m], 64, 2)
    side = sides(16, 0, 1)
    ds_ref[...] = side
    send(16, 0, df_ref[...], 128, 1)
    send(16, 128, side, 128, 1)
    dm_ref[...] = dc_ref[...] + sides(17, 64, 1)[0:64]
    send(17, 0, dm_ref[...], 64, 1)


def finish_kernel(
    lw_ref, acc, cf_ref, cs_ref, cm_ref, df_ref, ds_ref, dm_ref, fu_ref, fd_ref, fine_ref, coarse_ref,
    lw, vf, wf, vc, wc, tall, low, fine_out, coarse_out, sems, lw_sem,
):
    take = pltpu.make_async_copy(lw_ref, lw, lw_sem)
    take.start()
    a = iota((256, 256), 0)
    b = iota((256, 256), 1)
    place = ((b >> 7) == ((a >> 5) & 1)) & ((b & 127) == 1 + 4 * (a & 31) + (a >> 6))
    place = jnp.where(place, 1.0, 0.0).astype(BF)
    wide = sum(mm(p, place) for p in split3(acc[...]))
    far = jnp.abs(iota((128, 128), 0) - 2 * iota((128, 128), 1))
    halve = jnp.where(far == 0, 0.75, jnp.where(far == 1, 0.5, jnp.where(far == 2, 0.125, 0.0))).astype(BF)

    def apply(field, diag):
        rows, lanes = field.shape
        near = pltpu.roll(field, 1, 0) + pltpu.roll(field, rows - 1, 0)
        near = near + (pltpu.roll(field, 1, 1) + pltpu.roll(field, lanes - 1, 1))
        return diag * field - near

    def twice(field, diag):
        first = jnp.where(diag > 0.0, apply(field, diag), 0.0)
        return apply(first, diag)

    def rim(scratch, size, row, width, lanes):
        last = scratch.shape[0]
        scratch[size:last, :] = jnp.zeros((last - size, lanes), F)
        scratch[size:size + width, :] = fd_ref[row:row + width, 0:lanes]
        scratch[last - width:last, :] = fu_ref[row:row + width, 0:lanes]

    wf[0:128, 0:128] = df_ref[...]
    wf[0:128, 128:256] = ds_ref[...]
    rim(wf, 128, 16, 1, 256)
    wc[0:64, :] = dm_ref[...]
    rim(wc, 64, 17, 1, 128)
    for m in range(4):
        vf[m, 0:128, 0:128] = cf_ref[m]
        vf[m, 0:128, 128:256] = cs_ref[m]
        rim(vf.at[m], 128, 2 * m, 2, 256)
        vc[m, 0:64, :] = cm_ref[m]
        rim(vc.at[m], 64, 8 + 2 * m, 2, 128)
    take.wait()
    sends = []
    for m in range(4):
        tall[m, 0:16, :] = jnp.zeros((16, 128), F)
        tall[m, 72:144, :] = jnp.zeros((72, 128), F)
        for h in range(2):
            for r in range(4):
                at = m * 64 + r * 16
                spots = pl.ds(9 + 61 * h + r, 16, stride=4)
                part = wide[at:at + 16, h * 128:(h + 1) * 128]
                tall[m, spots, :] = part if h == 0 else part + tall[m, spots, :]
        every = [tall[m, pl.ds(8 + k, 64, stride=2), :] for k in range(-2, 3)]
        low[m * 64:(m + 1) * 64, :] = 0.75 * every[2] + 0.5 * (every[1] + every[3]) + 0.125 * (every[0] + every[4])
        fine_out[m] = lw[0] * tall[m, 8:136, :] - twice(vf[m], wf[...])[0:128, 0:128]
        send = pltpu.make_async_copy(fine_out.at[m], fine_ref.at[m], sems.at[m])
        send.start()
        sends.append(send)
    coarse = sum(mm(p, halve) for p in split3(low[...]))
    for m in range(4):
        coarse_out[m] = lw[1] * coarse[m * 64:(m + 1) * 64, 0:64] - twice(vc[m], wc[...])[0:64, 0:64]
    send = pltpu.make_async_copy(coarse_out, coarse_ref, sems.at[4])
    send.start()
    for send in sends + [send]:
        send.wait()


def neighbours(axis):
    count = lax.axis_size(axis)
    up = [(i, i + 1) for i in range(count - 1)]
    return up, [(j, i) for i, j in up]


def edges(coef_fine, coef_coarse, kappa_map, kappa_table, at):
    smem = pl.BlockSpec(memory_space=pltpu.SMEM)
    vmem = pl.BlockSpec(memory_space=pltpu.VMEM)
    square = pltpu.VMEM((128, 128), F)
    to_left, to_right, df, dc = pl.pallas_call(
        columns_kernel,
        in_specs=[smem] + [vmem] * 3,
        out_shape=[struct(24, 128), struct(24, 128), struct(128, 128), struct(64, 128)],
        scratch_shapes=[square],
        compiler_params=params(),
        name="edge_columns",
    )(kappa_table, coef_fine, coef_coarse, kappa_map)
    onward, back = neighbours("tx")
    from_left = lax.ppermute(to_right, "tx", onward)
    from_right = lax.ppermute(to_left, "tx", back)
    to_up, to_down, side, coarse, dside, dcoarse = pl.pallas_call(
        rows_kernel,
        in_specs=[vmem] * 6 + [pl.BlockSpec(memory_space=pl.ANY)],
        out_shape=[struct(24, 256), struct(24, 256), struct(4, 128, 128), struct(4, 64, 128), struct(128, 128), struct(64, 128)],
        scratch_shapes=[square],
        compiler_params=params(),
        name="edge_rows",
    )(coef_fine, coef_coarse, df, dc, from_left, from_right, at)
    onward, back = neighbours("ty")
    from_up = lax.ppermute(to_down, "ty", onward)
    from_down = lax.ppermute(to_up, "ty", back)
    return coef_fine, side, coarse, df, dside, dcoarse, from_up, from_down


def finish(level_weight, total, fields):
    vmem = pl.BlockSpec(memory_space=pltpu.VMEM)
    return pl.pallas_call(
        finish_kernel,
        in_specs=[pl.BlockSpec(memory_space=pl.ANY)] + [vmem] * (1 + len(fields)),
        out_specs=[pl.BlockSpec(memory_space=pl.ANY)] * 2,
        out_shape=[struct(4, 128, 128), struct(4, 64, 64)],
        scratch_shapes=[
            pltpu.SMEM((2,), F),
            pltpu.VMEM((4, 136, 256), F),
            pltpu.VMEM((136, 256), F),
            pltpu.VMEM((4, 72, 128), F),
            pltpu.VMEM((72, 128), F),
            pltpu.VMEM((4, 144, 128), F),
            pltpu.VMEM((256, 128), F),
            pltpu.VMEM((4, 128, 128), F),
            pltpu.VMEM((4, 64, 64), F),
            pltpu.SemaphoreType.DMA((5,)),
            pltpu.SemaphoreType.DMA,
        ],
        compiler_params=params(),
        name="finish_tiles",
    )(level_weight, total, *fields)


def spline(t):
    s = 1.0 - t
    return (
        s * s * s / 6.0,
        (3.0 * t * t * t - 6.0 * t * t + 4.0) / 6.0,
        (-3.0 * t * t * t + 3.0 * t * t + 3.0 * t + 1.0) / 6.0,
        t * t * t / 6.0,
    )


def rotate(weights, start):
    odd = (start & 1) == 1
    weights = [jnp.where(odd, weights[(r - 1) % 4], weights[r]) for r in range(4)]
    two = (start & 2) == 2
    return [jnp.where(two, weights[(r - 2) % 4], weights[r]) for r in range(4)]


def place_kernel(off_ref, pos_ref, out_ref):
    sy = off_ref[0] - 2
    sx = off_ref[1] - 2
    upper = sy >= 61
    sy = jnp.where(upper, sy - 61, sy)
    by = sy & 3
    bx = sx & 3
    qy = sy >> 2
    qx = (sx >> 2) + jnp.where(upper, 32, 0)
    wy = rotate(spline(pos_ref[0]), by)
    wx = rotate(spline(pos_ref[1]), bx)
    for r in range(4):
        out_ref[r] = (qy + jnp.where(by > r, 1, 0)).astype(F)
        out_ref[4 + r] = (qx + jnp.where(bx > r, 1, 0)).astype(F)
        out_ref[8 + r] = wx[r]
        out_ref[12 + r] = wy[r]


def places(offsets, positions):
    tiles, slots = offsets.shape[1:]
    group = 16
    points = pl.BlockSpec((2, group, slots), lambda i: (0, i, 0))
    return pl.pallas_call(
        place_kernel,
        grid=(tiles // group,),
        in_specs=[points, points],
        out_specs=pl.BlockSpec((16, group, slots), lambda i: (0, i, 0)),
        out_shape=struct(16, tiles, slots),
        compiler_params=params(),
        name="place_rows",
    )(offsets, positions)


def project_kernel(group, slots, v_ref, at_ref, acc, values):
    @pl.when(pl.program_id(0) == 0)
    def _():
        acc[...] = jnp.zeros_like(acc)

    chunks = slots // 128
    for m in range(4):
        v = jnp.concatenate([v_ref[pl.ds(4 * kc + m, group, stride=4 * chunks), :] for kc in range(chunks)], 1)
        for r in range(4):
            values[4 * m + r] = v * at_ref[12 + r]
    i16 = iota((16, slots), 0).astype(F).astype(BF)
    i64 = iota((64, slots), 0).astype(F).astype(BF)
    zero = jnp.zeros((), BF)

    def spread(ref, i, s, n):
        row = jnp.broadcast_to(ref[i, pl.ds(s, 1), :], (16, slots)).astype(BF)
        return jnp.broadcast_to(row[None], (n // 16, 16, slots)).reshape(n, slots)

    def build(s):
        left = [None] * 16
        for r in range(4):
            here = i16 == spread(at_ref, r, s, 16)
            for m in range(4):
                left[4 * m + r] = jnp.where(here, spread(values, 4 * m + r, s, 16), zero)
        right = [jnp.where(i64 == spread(at_ref, 4 + r, s, 64), spread(at_ref, 8 + r, s, 64), zero) for r in range(4)]
        return jnp.concatenate(left, 0), jnp.concatenate(right, 0)

    for s in range(group):
        left, right = build(s)
        acc[...] += mm(left, right, ((1,), (1,)))


def project(values, at):
    tiles, slots = at.shape[1:]
    group = 32
    return pl.pallas_call(
        functools.partial(project_kernel, group, slots),
        grid=(tiles // group,),
        in_specs=[
            pl.BlockSpec((group * slots // 32, 128), lambda i: (i, 0)),
            pl.BlockSpec((16, group, slots), lambda i: (0, i, 0)),
        ],
        out_specs=pl.BlockSpec((256, 256), lambda i: (0, 0)),
        out_shape=struct(256, 256),
        scratch_shapes=[pltpu.VMEM((16, group, slots), F)],
        compiler_params=params(),
        name="project_rows",
    )(values, at)


def on_device(residual, counts, offsets, positions, coef_fine, coef_coarse, kappa_map, kappa_table, level_weight):
    tiles = residual.shape[2]
    packed = pack(counts, residual[0]).reshape(tiles, -1, 4, 128)
    values = lax.all_to_all(packed, AXES, split_axis=0, concat_axis=0, tiled=True).reshape(-1, 128)
    at = places(offsets[0], positions[0])
    fields = edges(coef_fine, coef_coarse, kappa_map, kappa_table, at)
    return tuple(finish(level_weight, project(values, at), fields))


def solution(mesh):
    rows = P(AXES, None, None, None)
    tile = P(None, "ty", "tx")
    return jax.shard_map(
        on_device,
        mesh=mesh,
        in_specs=(rows, P(AXES, None), rows, rows, tile, tile, P("ty", "tx"), P(), P()),
        out_specs=(tile, tile),
        check_vma=False,
    )
```

```python
import functools

import jax
import jax.numpy as jnp
from jax import lax
from jax.experimental import pallas as pl
from jax.experimental.pallas import tpu as pltpu
from jax.sharding import PartitionSpec as P

BF = jnp.bfloat16
F = jnp.float32
VMEM_LIMIT = 48 * 1024 * 1024
AXES = ("ty", "tx")


def struct(*shape):
    return jax.ShapeDtypeStruct(shape, F)


def iota(shape, dim):
    return lax.broadcasted_iota(jnp.int32, shape, dim)


def mm(a, b, dims=((1,), (0,))):
    return lax.dot_general(a, b, (dims, ((), ())), preferred_element_type=F)


def split3(a):
    hi = a.astype(BF)
    a = a - hi.astype(F)
    mid = a.astype(BF)
    lo = (a - mid.astype(F)).astype(BF)
    return hi, mid, lo


def params():
    return pltpu.CompilerParams(vmem_limit_bytes=VMEM_LIMIT)


def pack_kernel(block, counts_ref, res_ref, out_ref, counts, loaded, built, sems, out_sems, count_sem):
    tiles, slots = res_ref.shape[1:]
    parts = tiles // block
    chunks = slots // 128
    rows = 4 * chunks * block
    take = pltpu.make_async_copy(counts_ref, counts, count_sem)
    take.start()
    loads = [
        pltpu.make_async_copy(res_ref.at[:, pl.ds(i * block, block), :], loaded.at[i], sems.at[i]) for i in range(parts)
    ]
    for load in loads:
        load.start()
    take.wait()
    stores = []
    for i in range(parts):
        loads[i].wait()
        for d in range(0, block, 8):
            live = jnp.zeros((8, 128), jnp.int32)
            for j in range(8):
                live = jnp.where(iota((8, 128), 0) == j, counts[0, i * block + d + j], live)
            for kc in range(chunks):
                keep = iota((8, 128), 1) + 128 * kc < live
                for m in range(4):
                    row = (d * chunks + kc) * 4 + m
                    value = jnp.where(keep, loaded[i, m, d:d + 8, 128 * kc:128 * kc + 128], 0.0)
                    built[i, pl.ds(row, 8, stride=4 * chunks), :] = value
        store = pltpu.make_async_copy(built.at[i], out_ref.at[pl.ds(i * rows, rows), :], out_sems.at[i])
        store.start()
        stores.append(store)
    for store in stores:
        store.wait()


def pack(counts, residual):
    channels, tiles, slots = residual.shape
    block = 32
    parts = tiles // block
    rows = 4 * (slots // 128)
    return pl.pallas_call(
        functools.partial(pack_kernel, block),
        in_specs=[pl.BlockSpec(memory_space=pltpu.HBM)] * 2,
        out_specs=pl.BlockSpec(memory_space=pl.ANY),
        out_shape=struct(tiles * rows, 128),
        scratch_shapes=[
            pltpu.SMEM((1, tiles), jnp.int32),
            pltpu.VMEM((parts, channels, block, slots), F),
            pltpu.VMEM((parts, block * rows, 128), F),
            pltpu.SemaphoreType.DMA((parts,)),
            pltpu.SemaphoreType.DMA((parts,)),
            pltpu.SemaphoreType.DMA,
        ],
        compiler_params=pltpu.CompilerParams(vmem_limit_bytes=62 * 1024 * 1024),
        name="pack_rows",
    )(counts, residual)


def classes_to_diag(kinds, table_ref, level):
    total = jnp.zeros(kinds.shape, F)
    for k in range(table_ref.shape[1]):
        total = jnp.where(kinds == k, table_ref[level, k], total)
    return 4.0 + total


def is_odd(axis):
    return (lax.axis_index(axis) & 1) == 1


def columns_kernel(table_ref, cf_ref, cc_ref, km_ref, with_ref, off_ref, df_ref, dc_ref, square):
    odd = is_odd("tx")
    with_ref[...] = jnp.zeros_like(with_ref)
    off_ref[...] = jnp.zeros_like(off_ref)
    square[...] = jnp.zeros_like(square)
    df = classes_to_diag(km_ref[...], table_ref, 0)
    df_ref[...] = df
    even = km_ref[pl.ds(0, 64, stride=2), :].astype(F).astype(BF)
    pick = jnp.where(iota((128, 128), 0) == 2 * iota((128, 128), 1), 1.0, 0.0).astype(BF)
    dc = classes_to_diag(mm(even, pick).astype(jnp.int32), table_ref, 1)
    dc = jnp.where(iota((64, 128), 1) < 64, dc, 0.0)
    dc_ref[...] = dc

    def send(row, turned, size, width):
        low, high = turned[0:width], turned[size - width:size]
        with_ref[pl.ds(row, width), :] = jnp.where(odd, low, high)
        off_ref[pl.ds(row, width), :] = jnp.where(odd, high, low)

    for m in range(4):
        send(2 * m, cf_ref[m].T, 128, 2)
        square[0:64, 0:64] = cc_ref[m]
        send(8 + 2 * m, square[...].T, 64, 2)
    send(16, df.T, 128, 1)
    square[0:64, :] = dc
    send(17, square[...].T, 64, 1)


def cross(field):
    rows, lanes = field.shape
    near = pltpu.roll(field, 1, 1) + pltpu.roll(field, lanes - 1, 1)
    return near + (pltpu.roll(field, 1, 0) + pltpu.roll(field, rows - 1, 0))


def rows_kernel(
    cf_ref, cc_ref, df_ref, dc_ref, fw_ref, fo_ref, at_ref, with_ref, off_ref, bf_ref, bc_ref, square, vf, wf, vc, wc
):
    odd_x, odd_y = is_odd("tx"), is_odd("ty")
    with_ref[...] = jnp.zeros_like(with_ref)
    off_ref[...] = jnp.zeros_like(off_ref)
    left = jnp.where(odd_x, fw_ref[...], fo_ref[...])
    right = jnp.where(odd_x, fo_ref[...], fw_ref[...])

    def sides(row, first, width):
        square[...] = jnp.zeros_like(square)
        square[first:first + width, :] = right[row:row + width, :]
        square[128 - width:128, :] = left[row:row + width, :]
        return square[...].T

    def send(row, field, size, width):
        lanes = field.shape[1]
        low, high = field[0:width], field[size - width:size]
        with_ref[pl.ds(row, width), 0:lanes] = jnp.where(odd_y, low, high)
        off_ref[pl.ds(row, width), 0:lanes] = jnp.where(odd_y, high, low)

    def twice(field, diag):
        first = jnp.where(diag > 0.0, diag * field - cross(field), 0.0)
        return diag * first - cross(first)

    wf[...] = jnp.zeros_like(wf)
    wf[0:128, 0:128] = df_ref[...]
    wf[0:128, 128:256] = sides(16, 0, 1)
    send(16, wf[...], 128, 1)
    wc[...] = jnp.zeros_like(wc)
    wc[0:64, :] = dc_ref[...] + sides(17, 64, 1)[0:64]
    send(17, wc[...], 64, 1)
    for m in range(4):
        vf[m, 128:136, :] = jnp.zeros((8, 256), F)
        vf[m, 0:128, 0:128] = cf_ref[m]
        vf[m, 0:128, 128:256] = sides(2 * m, 0, 2)
        send(2 * m, vf[m], 128, 2)
        vc[m, 64:72, :] = jnp.zeros((8, 128), F)
        vc[m, 0:64, :] = sides(8 + 2 * m, 64, 2)[0:64]
        vc[m, 0:64, 0:64] = cc_ref[m]
        send(8 + 2 * m, vc[m], 64, 2)
    for m in range(4):
        bf_ref[m] = twice(vf[m], wf[...])[0:128, 0:128]
        bc_ref[m] = twice(vc[m], wc[...])[0:64, :]


def rim(own, other, rows, diag, lanes, step):
    here = own[diag:diag + 1, 0:lanes]
    there = other[diag:diag + 1, 0:lanes]
    near = other[rows:rows + 8, 0:lanes]
    far = pltpu.roll(near, step, 0)
    edge = pltpu.roll(own[rows:rows + 8, 0:lanes], step, 0)

    def sideways(x):
        return pltpu.roll(x, 1, 1) + pltpu.roll(x, lanes - 1, 1)

    change = jnp.where(here > 0.0, -near, 0.0)
    beyond = jnp.where(there > 0.0, there * near - (far + edge + sideways(near)), 0.0)
    return here * change - sideways(change) - beyond, -change


def finish_kernel(
    lw_ref, acc, bf_ref, bc_ref, with_ref, off_ref, fw_ref, fo_ref, fine_ref, coarse_ref,
    lw, tall, low, fine_out, coarse_out, sems, lw_sem,
):
    take = pltpu.make_async_copy(lw_ref, lw, lw_sem)
    take.start()
    a = iota((256, 256), 0)
    b = iota((256, 256), 1)
    place = ((b >> 7) == ((a >> 5) & 1)) & ((b & 127) == 1 + 4 * (a & 31) + (a >> 6))
    place = jnp.where(place, 1.0, 0.0).astype(BF)
    wide = sum(mm(p, place) for p in split3(acc[...]))
    far = jnp.abs(iota((128, 128), 0) - 2 * iota((128, 128), 1))
    halve = jnp.where(far == 0, 0.75, jnp.where(far == 1, 0.5, jnp.where(far == 2, 0.125, 0.0))).astype(BF)

    def edges(out, m, size, width, above, below):
        for row, (both, at) in ((0, (above, 2 * m + 1)), (size - 1, (below, 2 * m))):
            inner = 1 if row == 0 else size - 2
            out[m, row:row + 1, :] = out[m, row:row + 1, :] - both[0][at:at + 1, 0:width]
            out[m, inner:inner + 1, :] = out[m, inner:inner + 1, :] - both[1][at:at + 1, 0:width]

    odd = is_odd("ty")
    top = jnp.where(odd, with_ref[...], off_ref[...])
    bottom = jnp.where(odd, off_ref[...], with_ref[...])
    before = jnp.where(odd, fw_ref[...], fo_ref[...])
    after = jnp.where(odd, fo_ref[...], fw_ref[...])
    above = rim(top, before, 0, 16, 256, 1)
    below = rim(bottom, after, 0, 16, 256, 7)
    coarse_above = rim(top, before, 8, 17, 128, 1)
    coarse_below = rim(bottom, after, 8, 17, 128, 7)
    take.wait()
    sends = []
    for m in range(4):
        tall[m, 0:16, :] = jnp.zeros((16, 128), F)
        tall[m, 72:144, :] = jnp.zeros((72, 128), F)
        for h in range(2):
            for r in range(4):
                at = m * 64 + r * 16
                spots = pl.ds(9 + 61 * h + r, 16, stride=4)
                part = wide[at:at + 16, h * 128:(h + 1) * 128]
                tall[m, spots, :] = part if h == 0 else part + tall[m, spots, :]
        every = [tall[m, pl.ds(8 + k, 64, stride=2), :] for k in range(-2, 3)]
        low[m * 64:(m + 1) * 64, :] = 0.75 * every[2] + 0.5 * (every[1] + every[3]) + 0.125 * (every[0] + every[4])
        fine_out[m] = lw[0] * tall[m, 8:136, :] - bf_ref[m]
        edges(fine_out, m, 128, 128, above, below)
        send = pltpu.make_async_copy(fine_out.at[m], fine_ref.at[m], sems.at[m])
        send.start()
        sends.append(send)
    coarse = sum(mm(p, halve) for p in split3(low[...]))
    for m in range(4):
        coarse_out[m] = lw[1] * coarse[m * 64:(m + 1) * 64, 0:64] - bc_ref[m, :, 0:64]
        edges(coarse_out, m, 64, 64, coarse_above, coarse_below)
    send = pltpu.make_async_copy(coarse_out, coarse_ref, sems.at[4])
    send.start()
    for send in sends + [send]:
        send.wait()


def swap(x, axis, first):
    pairs = [(i, i + 1) for i in range(first, lax.axis_size(axis) - 1, 2)]
    return lax.ppermute(x, axis, pairs + [(j, i) for i, j in pairs])


def edges(coef_fine, coef_coarse, kappa_map, kappa_table, at):
    smem = pl.BlockSpec(memory_space=pltpu.SMEM)
    vmem = pl.BlockSpec(memory_space=pltpu.VMEM)
    square = pltpu.VMEM((128, 128), F)
    with_x, off_x, df, dc = pl.pallas_call(
        columns_kernel,
        in_specs=[smem] + [vmem] * 3,
        out_shape=[struct(24, 128), struct(24, 128), struct(128, 128), struct(64, 128)],
        scratch_shapes=[square],
        compiler_params=params(),
        name="edge_columns",
    )(kappa_table, coef_fine, coef_coarse, kappa_map)
    from_with = swap(with_x, "tx", 0)
    from_off = swap(off_x, "tx", 1)
    with_y, off_y, fine, coarse = pl.pallas_call(
        rows_kernel,
        in_specs=[vmem] * 6 + [pl.BlockSpec(memory_space=pl.ANY)],
        out_shape=[struct(24, 256), struct(24, 256), struct(4, 128, 128), struct(4, 64, 128)],
        scratch_shapes=[
            square,
            pltpu.VMEM((4, 136, 256), F),
            pltpu.VMEM((136, 256), F),
            pltpu.VMEM((4, 72, 128), F),
            pltpu.VMEM((72, 128), F),
        ],
        compiler_params=params(),
        name="edge_rows",
    )(coef_fine, coef_coarse, df, dc, from_with, from_off, at)
    return fine, coarse, with_y, off_y, swap(with_y, "ty", 0), swap(off_y, "ty", 1)


def finish(level_weight, total, fields):
    vmem = pl.BlockSpec(memory_space=pltpu.VMEM)
    return pl.pallas_call(
        finish_kernel,
        in_specs=[pl.BlockSpec(memory_space=pl.ANY)] + [vmem] * (1 + len(fields)),
        out_specs=[pl.BlockSpec(memory_space=pl.ANY)] * 2,
        out_shape=[struct(4, 128, 128), struct(4, 64, 64)],
        scratch_shapes=[
            pltpu.SMEM((2,), F),
            pltpu.VMEM((4, 144, 128), F),
            pltpu.VMEM((256, 128), F),
            pltpu.VMEM((4, 128, 128), F),
            pltpu.VMEM((4, 64, 64), F),
            pltpu.SemaphoreType.DMA((5,)),
            pltpu.SemaphoreType.DMA,
        ],
        compiler_params=params(),
        name="finish_tiles",
    )(level_weight, total, *fields)


def spline(t):
    s = 1.0 - t
    return (
        s * s * s / 6.0,
        (3.0 * t * t * t - 6.0 * t * t + 4.0) / 6.0,
        (-3.0 * t * t * t + 3.0 * t * t + 3.0 * t + 1.0) / 6.0,
        t * t * t / 6.0,
    )


def rotate(weights, start):
    odd = (start & 1) == 1
    weights = [jnp.where(odd, weights[(r - 1) % 4], weights[r]) for r in range(4)]
    two = (start & 2) == 2
    return [jnp.where(two, weights[(r - 2) % 4], weights[r]) for r in range(4)]


def place_kernel(off_ref, pos_ref, out_ref):
    sy = off_ref[0] - 2
    sx = off_ref[1] - 2
    upper = sy >= 61
    sy = jnp.where(upper, sy - 61, sy)
    by = sy & 3
    bx = sx & 3
    qy = sy >> 2
    qx = (sx >> 2) + jnp.where(upper, 32, 0)
    wy = rotate(spline(pos_ref[0]), by)
    wx = rotate(spline(pos_ref[1]), bx)
    for r in range(4):
        out_ref[r] = (qy + jnp.where(by > r, 1, 0)).astype(F)
        out_ref[4 + r] = (qx + jnp.where(bx > r, 1, 0)).astype(F)
        out_ref[8 + r] = wx[r]
        out_ref[12 + r] = wy[r]


def places(offsets, positions):
    tiles, slots = offsets.shape[1:]
    group = 16
    points = pl.BlockSpec((2, group, slots), lambda i: (0, i, 0))
    return pl.pallas_call(
        place_kernel,
        grid=(tiles // group,),
        in_specs=[points, points],
        out_specs=pl.BlockSpec((16, group, slots), lambda i: (0, i, 0)),
        out_shape=struct(16, tiles, slots),
        compiler_params=params(),
        name="place_rows",
    )(offsets, positions)


def project_kernel(group, slots, v_ref, at_ref, acc, values):
    @pl.when(pl.program_id(0) == 0)
    def _():
        acc[...] = jnp.zeros_like(acc)

    chunks = slots // 128
    for m in range(4):
        v = jnp.concatenate([v_ref[pl.ds(4 * kc + m, group, stride=4 * chunks), :] for kc in range(chunks)], 1)
        for r in range(4):
            values[4 * m + r] = v * at_ref[12 + r]
    i16 = iota((16, slots), 0).astype(F).astype(BF)
    i64 = iota((64, slots), 0).astype(F).astype(BF)
    zero = jnp.zeros((), BF)

    def spread(ref, i, s, n):
        row = jnp.broadcast_to(ref[i, pl.ds(s, 1), :], (16, slots)).astype(BF)
        return jnp.broadcast_to(row[None], (n // 16, 16, slots)).reshape(n, slots)

    def build(s):
        left = [None] * 16
        for r in range(4):
            here = i16 == spread(at_ref, r, s, 16)
            for m in range(4):
                left[4 * m + r] = jnp.where(here, spread(values, 4 * m + r, s, 16), zero)
        right = [jnp.where(i64 == spread(at_ref, 4 + r, s, 64), spread(at_ref, 8 + r, s, 64), zero) for r in range(4)]
        return jnp.concatenate(left, 0), jnp.concatenate(right, 0)

    for s in range(group):
        left, right = build(s)
        acc[...] += mm(left, right, ((1,), (1,)))


def project(values, at):
    tiles, slots = at.shape[1:]
    group = 32
    return pl.pallas_call(
        functools.partial(project_kernel, group, slots),
        grid=(tiles // group,),
        in_specs=[
            pl.BlockSpec((group * slots // 32, 128), lambda i: (i, 0)),
            pl.BlockSpec((16, group, slots), lambda i: (0, i, 0)),
        ],
        out_specs=pl.BlockSpec((256, 256), lambda i: (0, 0)),
        out_shape=struct(256, 256),
        scratch_shapes=[pltpu.VMEM((16, group, slots), F)],
        compiler_params=params(),
        name="project_rows",
    )(values, at)


def on_device(residual, counts, offsets, positions, coef_fine, coef_coarse, kappa_map, kappa_table, level_weight):
    tiles = residual.shape[2]
    packed = pack(counts, residual[0]).reshape(tiles, -1, 4, 128)
    values = lax.all_to_all(packed, AXES, split_axis=0, concat_axis=0, tiled=True).reshape(-1, 128)
    at = places(offsets[0], positions[0])
    fields = edges(coef_fine, coef_coarse, kappa_map, kappa_table, at)
    return tuple(finish(level_weight, project(values, at), fields))


def solution(mesh):
    rows = P(AXES, None, None, None)
    tile = P(None, "ty", "tx")
    return jax.shard_map(
        on_device,
        mesh=mesh,
        in_specs=(rows, P(AXES, None), rows, rows, tile, tile, P("ty", "tx"), P(), P()),
        out_specs=(tile, tile),
        check_vma=False,
    )
```

```python
import functools

import jax
import jax.numpy as jnp
from jax import lax
from jax.experimental import pallas as pl
from jax.experimental.pallas import tpu as pltpu
from jax.sharding import PartitionSpec as P

BF = jnp.bfloat16
F = jnp.float32
VMEM_LIMIT = 48 * 1024 * 1024
AXES = ("ty", "tx")


def struct(*shape):
    return jax.ShapeDtypeStruct(shape, F)


def iota(shape, dim):
    return lax.broadcasted_iota(jnp.int32, shape, dim)


def mm(a, b, dims=((1,), (0,))):
    return lax.dot_general(a, b, (dims, ((), ())), preferred_element_type=F)


def split3(a):
    hi = a.astype(BF)
    a = a - hi.astype(F)
    mid = a.astype(BF)
    lo = (a - mid.astype(F)).astype(BF)
    return hi, mid, lo


def params():
    return pltpu.CompilerParams(vmem_limit_bytes=VMEM_LIMIT)


def pack_kernel(block, counts_ref, res_ref, out_ref, counts, loaded, built, sems, out_sems, count_sem):
    tiles, slots = res_ref.shape[1:]
    parts = tiles // block
    chunks = slots // 128
    rows = 4 * chunks * block
    take = pltpu.make_async_copy(counts_ref, counts, count_sem)
    take.start()
    loads = [
        pltpu.make_async_copy(res_ref.at[:, pl.ds(i * block, block), :], loaded.at[i], sems.at[i]) for i in range(parts)
    ]
    for load in loads:
        load.start()
    take.wait()
    stores = []
    for i in range(parts):
        loads[i].wait()
        for d in range(0, block, 8):
            live = jnp.zeros((8, 128), jnp.int32)
            for j in range(8):
                live = jnp.where(iota((8, 128), 0) == j, counts[0, i * block + d + j], live)
            for kc in range(chunks):
                keep = iota((8, 128), 1) + 128 * kc < live
                for m in range(4):
                    row = (d * chunks + kc) * 4 + m
                    value = jnp.where(keep, loaded[i, m, d:d + 8, 128 * kc:128 * kc + 128], 0.0)
                    built[i, pl.ds(row, 8, stride=4 * chunks), :] = value
        store = pltpu.make_async_copy(built.at[i], out_ref.at[pl.ds(i * rows, rows), :], out_sems.at[i])
        store.start()
        stores.append(store)
    for store in stores:
        store.wait()


def pack(counts, residual):
    channels, tiles, slots = residual.shape
    block = 32
    parts = tiles // block
    rows = 4 * (slots // 128)
    return pl.pallas_call(
        functools.partial(pack_kernel, block),
        in_specs=[pl.BlockSpec(memory_space=pltpu.HBM)] * 2,
        out_specs=pl.BlockSpec(memory_space=pl.ANY),
        out_shape=struct(tiles * rows, 128),
        scratch_shapes=[
            pltpu.SMEM((1, tiles), jnp.int32),
            pltpu.VMEM((parts, channels, block, slots), F),
            pltpu.VMEM((parts, block * rows, 128), F),
            pltpu.SemaphoreType.DMA((parts,)),
            pltpu.SemaphoreType.DMA((parts,)),
            pltpu.SemaphoreType.DMA,
        ],
        compiler_params=pltpu.CompilerParams(vmem_limit_bytes=62 * 1024 * 1024),
        name="pack_rows",
    )(counts, residual)


def classes_to_diag(kinds, table_ref, level):
    total = jnp.zeros(kinds.shape, F)
    for k in range(table_ref.shape[1]):
        total = jnp.where(kinds == k, table_ref[level, k], total)
    return 4.0 + total


def is_odd(axis):
    return (lax.axis_index(axis) & 1) == 1


def columns_kernel(table_ref, cf_ref, cc_ref, km_ref, with_ref, off_ref, df_ref, dc_ref, square):
    odd = is_odd("tx")
    with_ref[...] = jnp.zeros_like(with_ref)
    off_ref[...] = jnp.zeros_like(off_ref)
    square[...] = jnp.zeros_like(square)
    df = classes_to_diag(km_ref[...], table_ref, 0)
    df_ref[...] = df
    even = km_ref[pl.ds(0, 64, stride=2), :].astype(F).astype(BF)
    pick = jnp.where(iota((128, 128), 0) == 2 * iota((128, 128), 1), 1.0, 0.0).astype(BF)
    dc = classes_to_diag(mm(even, pick).astype(jnp.int32), table_ref, 1)
    dc = jnp.where(iota((64, 128), 1) < 64, dc, 0.0)
    dc_ref[...] = dc

    def send(row, turned, size, width):
        low, high = turned[0:width], turned[size - width:size]
        with_ref[pl.ds(row, width), :] = jnp.where(odd, low, high)
        off_ref[pl.ds(row, width), :] = jnp.where(odd, high, low)

    for m in range(4):
        send(2 * m, cf_ref[m].T, 128, 2)
        square[0:64, 0:64] = cc_ref[m]
        send(8 + 2 * m, square[...].T, 64, 2)
    send(16, df.T, 128, 1)
    square[0:64, :] = dc
    send(17, square[...].T, 64, 1)


def cross(field):
    rows, lanes = field.shape
    near = pltpu.roll(field, 1, 1) + pltpu.roll(field, lanes - 1, 1)
    return near + (pltpu.roll(field, 1, 0) + pltpu.roll(field, rows - 1, 0))


def rows_kernel(
    cf_ref, cc_ref, df_ref, dc_ref, fw_ref, fo_ref, at_ref, with_ref, off_ref, bf_ref, bc_ref, square, vf, wf, vc, wc
):
    odd_x, odd_y = is_odd("tx"), is_odd("ty")
    with_ref[...] = jnp.zeros_like(with_ref)
    off_ref[...] = jnp.zeros_like(off_ref)
    left = jnp.where(odd_x, fw_ref[...], fo_ref[...])
    right = jnp.where(odd_x, fo_ref[...], fw_ref[...])

    def sides(row, first, width):
        square[...] = jnp.zeros_like(square)
        square[first:first + width, :] = right[row:row + width, :]
        square[128 - width:128, :] = left[row:row + width, :]
        return square[...].T

    def send(row, field, size, width):
        lanes = field.shape[1]
        low, high = field[0:width], field[size - width:size]
        with_ref[pl.ds(row, width), 0:lanes] = jnp.where(odd_y, low, high)
        off_ref[pl.ds(row, width), 0:lanes] = jnp.where(odd_y, high, low)

    def twice(field, diag):
        first = jnp.where(diag > 0.0, diag * field - cross(field), 0.0)
        return diag * first - cross(first)

    wf[...] = jnp.zeros_like(wf)
    wf[0:128, 0:128] = df_ref[...]
    wf[0:128, 128:256] = sides(16, 0, 1)
    send(16, wf[...], 128, 1)
    wc[...] = jnp.zeros_like(wc)
    wc[0:64, :] = dc_ref[...] + sides(17, 64, 1)[0:64]
    send(17, wc[...], 64, 1)
    for m in range(4):
        vf[m, 128:136, :] = jnp.zeros((8, 256), F)
        vf[m, 0:128, 0:128] = cf_ref[m]
        vf[m, 0:128, 128:256] = sides(2 * m, 0, 2)
        send(2 * m, vf[m], 128, 2)
        vc[m, 64:72, :] = jnp.zeros((8, 128), F)
        vc[m, 0:64, :] = sides(8 + 2 * m, 64, 2)[0:64]
        vc[m, 0:64, 0:64] = cc_ref[m]
        send(8 + 2 * m, vc[m], 64, 2)
    for m in range(4):
        bf_ref[m] = twice(vf[m], wf[...])[0:128, 0:128]
        bc_ref[m] = twice(vc[m], wc[...])[0:64, :]


def rim(own, other, rows, diag, lanes, step):
    here = own[diag:diag + 1, 0:lanes]
    there = other[diag:diag + 1, 0:lanes]
    near = other[rows:rows + 8, 0:lanes]
    far = pltpu.roll(near, step, 0)
    edge = pltpu.roll(own[rows:rows + 8, 0:lanes], step, 0)

    def sideways(x):
        return pltpu.roll(x, 1, 1) + pltpu.roll(x, lanes - 1, 1)

    change = jnp.where(here > 0.0, -near, 0.0)
    beyond = jnp.where(there > 0.0, there * near - (far + edge + sideways(near)), 0.0)
    return here * change - sideways(change) - beyond, -change


def finish_kernel(
    lw_ref, acc, bf_ref, bc_ref, with_ref, off_ref, fw_ref, fo_ref, fine_ref, coarse_ref,
    lw, tall, low, fine_out, coarse_out, sems, lw_sem,
):
    take = pltpu.make_async_copy(lw_ref, lw, lw_sem)
    take.start()
    a = iota((256, 256), 0)
    b = iota((256, 256), 1)
    place = ((b >> 7) == ((a >> 5) & 1)) & ((b & 127) == 1 + 4 * (a & 31) + (a >> 6))
    place = jnp.where(place, 1.0, 0.0).astype(BF)
    wide = sum(mm(p, place) for p in split3(acc[...]))
    far = jnp.abs(iota((128, 128), 0) - 2 * iota((128, 128), 1))
    halve = jnp.where(far == 0, 0.75, jnp.where(far == 1, 0.5, jnp.where(far == 2, 0.125, 0.0))).astype(BF)

    def edges(out, m, size, width, above, below):
        for row, (both, at) in ((0, (above, 2 * m + 1)), (size - 1, (below, 2 * m))):
            inner = 1 if row == 0 else size - 2
            out[m, row:row + 1, :] = out[m, row:row + 1, :] - both[0][at:at + 1, 0:width]
            out[m, inner:inner + 1, :] = out[m, inner:inner + 1, :] - both[1][at:at + 1, 0:width]

    odd = is_odd("ty")
    top = jnp.where(odd, with_ref[...], off_ref[...])
    bottom = jnp.where(odd, off_ref[...], with_ref[...])
    before = jnp.where(odd, fw_ref[...], fo_ref[...])
    after = jnp.where(odd, fo_ref[...], fw_ref[...])
    above = rim(top, before, 0, 16, 256, 1)
    below = rim(bottom, after, 0, 16, 256, 7)
    coarse_above = rim(top, before, 8, 17, 128, 1)
    coarse_below = rim(bottom, after, 8, 17, 128, 7)
    take.wait()
    sends = []
    for m in range(4):
        tall[m, 0:16, :] = jnp.zeros((16, 128), F)
        tall[m, 72:144, :] = jnp.zeros((72, 128), F)
        for h in range(2):
            for r in range(4):
                at = m * 64 + r * 16
                spots = pl.ds(9 + 61 * h + r, 16, stride=4)
                part = wide[at:at + 16, h * 128:(h + 1) * 128]
                tall[m, spots, :] = part if h == 0 else part + tall[m, spots, :]
        every = [tall[m, pl.ds(8 + k, 64, stride=2), :] for k in range(-2, 3)]
        low[m * 64:(m + 1) * 64, :] = 0.75 * every[2] + 0.5 * (every[1] + every[3]) + 0.125 * (every[0] + every[4])
        fine_out[m] = lw[0] * tall[m, 8:136, :] - bf_ref[m]
        edges(fine_out, m, 128, 128, above, below)
        send = pltpu.make_async_copy(fine_out.at[m], fine_ref.at[m], sems.at[m])
        send.start()
        sends.append(send)
    coarse = sum(mm(p, halve) for p in split3(low[...]))
    for m in range(4):
        coarse_out[m] = lw[1] * coarse[m * 64:(m + 1) * 64, 0:64] - bc_ref[m, :, 0:64]
        edges(coarse_out, m, 64, 64, coarse_above, coarse_below)
    send = pltpu.make_async_copy(coarse_out, coarse_ref, sems.at[4])
    send.start()
    for send in sends + [send]:
        send.wait()


def swap(x, axis, first):
    pairs = [(i, i + 1) for i in range(first, lax.axis_size(axis) - 1, 2)]
    return lax.ppermute(x, axis, pairs + [(j, i) for i, j in pairs])


def edges(coef_fine, coef_coarse, kappa_map, kappa_table, at):
    smem = pl.BlockSpec(memory_space=pltpu.SMEM)
    vmem = pl.BlockSpec(memory_space=pltpu.VMEM)
    square = pltpu.VMEM((128, 128), F)
    with_x, off_x, df, dc = pl.pallas_call(
        columns_kernel,
        in_specs=[smem] + [vmem] * 3,
        out_shape=[struct(24, 128), struct(24, 128), struct(128, 128), struct(64, 128)],
        scratch_shapes=[square],
        compiler_params=params(),
        name="edge_columns",
    )(kappa_table, coef_fine, coef_coarse, kappa_map)
    from_with = swap(with_x, "tx", 0)
    from_off = swap(off_x, "tx", 1)
    with_y, off_y, fine, coarse = pl.pallas_call(
        rows_kernel,
        in_specs=[vmem] * 6 + [pl.BlockSpec(memory_space=pl.ANY)],
        out_shape=[struct(24, 256), struct(24, 256), struct(4, 128, 128), struct(4, 64, 128)],
        scratch_shapes=[
            square,
            pltpu.VMEM((4, 136, 256), F),
            pltpu.VMEM((136, 256), F),
            pltpu.VMEM((4, 72, 128), F),
            pltpu.VMEM((72, 128), F),
        ],
        compiler_params=params(),
        name="edge_rows",
    )(coef_fine, coef_coarse, df, dc, from_with, from_off, at)
    return fine, coarse, with_y, off_y, swap(with_y, "ty", 0), swap(off_y, "ty", 1)


def finish(level_weight, total, fields):
    vmem = pl.BlockSpec(memory_space=pltpu.VMEM)
    return pl.pallas_call(
        finish_kernel,
        in_specs=[pl.BlockSpec(memory_space=pl.ANY)] + [vmem] * (1 + len(fields)),
        out_specs=[pl.BlockSpec(memory_space=pl.ANY)] * 2,
        out_shape=[struct(4, 128, 128), struct(4, 64, 64)],
        scratch_shapes=[
            pltpu.SMEM((2,), F),
            pltpu.VMEM((4, 144, 128), F),
            pltpu.VMEM((256, 128), F),
            pltpu.VMEM((4, 128, 128), F),
            pltpu.VMEM((4, 64, 64), F),
            pltpu.SemaphoreType.DMA((5,)),
            pltpu.SemaphoreType.DMA,
        ],
        compiler_params=params(),
        name="finish_tiles",
    )(level_weight, total, *fields)


def spline(t):
    s = 1.0 - t
    return (
        s * s * s / 6.0,
        (3.0 * t * t * t - 6.0 * t * t + 4.0) / 6.0,
        (-3.0 * t * t * t + 3.0 * t * t + 3.0 * t + 1.0) / 6.0,
        t * t * t / 6.0,
    )


def rotate(weights, start):
    odd = (start & 1) == 1
    weights = [jnp.where(odd, weights[(r - 1) % 4], weights[r]) for r in range(4)]
    two = (start & 2) == 2
    return [jnp.where(two, weights[(r - 2) % 4], weights[r]) for r in range(4)]


def place_kernel(off_ref, pos_ref, out_ref):
    sy = off_ref[0] - 2
    sx = off_ref[1] - 2
    upper = sy >= 61
    sy = jnp.where(upper, sy - 61, sy)
    by = sy & 3
    bx = sx & 3
    qy = sy >> 2
    qx = (sx >> 2) + jnp.where(upper, 32, 0)
    wy = rotate(spline(pos_ref[0]), by)
    wx = rotate(spline(pos_ref[1]), bx)
    for r in range(4):
        out_ref[r] = (qy + jnp.where(by > r, 1, 0)).astype(F)
        out_ref[4 + r] = (qx + jnp.where(bx > r, 1, 0)).astype(F)
        out_ref[8 + r] = wx[r]
        out_ref[12 + r] = wy[r]


def places(offsets, positions):
    tiles, slots = offsets.shape[1:]
    group = 16
    points = pl.BlockSpec((2, group, slots), lambda i: (0, i, 0))
    return pl.pallas_call(
        place_kernel,
        grid=(tiles // group,),
        in_specs=[points, points],
        out_specs=pl.BlockSpec((16, group, slots), lambda i: (0, i, 0)),
        out_shape=struct(16, tiles, slots),
        compiler_params=params(),
        name="place_rows",
    )(offsets, positions)


def project_kernel(group, slots, v_ref, at_ref, acc, values):
    @pl.when(pl.program_id(0) == 0)
    def _():
        acc[...] = jnp.zeros_like(acc)

    chunks = slots // 128
    base = pl.multiple_of(pl.program_id(0) * (group * 4 * chunks), group * 4 * chunks)

    def weigh(first, m):
        rows = [v_ref[pl.ds(base + (first * chunks + kc) * 4 + m, 8, stride=4 * chunks), :] for kc in range(chunks)]
        v = jnp.concatenate(rows, 1)
        for r in range(4):
            values[4 * m + r, first:first + 8, :] = v * at_ref[12 + r, first:first + 8, :]

    for m in range(4):
        weigh(0, m)
    i16 = iota((16, slots), 0).astype(F).astype(BF)
    i64 = iota((64, slots), 0).astype(F).astype(BF)
    zero = jnp.zeros((), BF)

    def spread(ref, i, s, n):
        row = jnp.broadcast_to(ref[i, pl.ds(s, 1), :], (16, slots)).astype(BF)
        return jnp.broadcast_to(row[None], (n // 16, 16, slots)).reshape(n, slots)

    def build(s):
        left = [None] * 16
        for r in range(4):
            here = i16 == spread(at_ref, r, s, 16)
            for m in range(4):
                left[4 * m + r] = jnp.where(here, spread(values, 4 * m + r, s, 16), zero)
        right = [jnp.where(i64 == spread(at_ref, 4 + r, s, 64), spread(at_ref, 8 + r, s, 64), zero) for r in range(4)]
        return jnp.concatenate(left, 0), jnp.concatenate(right, 0)

    for s in range(group):
        if s + 8 < group and s % 2 == 1:
            weigh(s // 8 * 8 + 8, s % 8 // 2)
        left, right = build(s)
        acc[...] += mm(left, right, ((1,), (1,)))


def project(values, at):
    tiles, slots = at.shape[1:]
    group = 32
    return pl.pallas_call(
        functools.partial(project_kernel, group, slots),
        grid=(tiles // group,),
        in_specs=[
            pl.BlockSpec(memory_space=pltpu.VMEM),
            pl.BlockSpec((16, group, slots), lambda i: (0, i, 0)),
        ],
        out_specs=pl.BlockSpec((256, 256), lambda i: (0, 0)),
        out_shape=struct(256, 256),
        scratch_shapes=[pltpu.VMEM((16, group, slots), F)],
        compiler_params=params(),
        name="project_rows",
    )(values, at)


def on_device(residual, counts, offsets, positions, coef_fine, coef_coarse, kappa_map, kappa_table, level_weight):
    tiles = residual.shape[2]
    packed = pack(counts, residual[0]).reshape(tiles, -1, 4, 128)
    values = lax.all_to_all(packed, AXES, split_axis=0, concat_axis=0, tiled=True).reshape(-1, 128)
    at = places(offsets[0], positions[0])
    fields = edges(coef_fine, coef_coarse, kappa_map, kappa_table, at)
    return tuple(finish(level_weight, project(values, at), fields))


def solution(mesh):
    rows = P(AXES, None, None, None)
    tile = P(None, "ty", "tx")
    return jax.shard_map(
        on_device,
        mesh=mesh,
        in_specs=(rows, P(AXES, None), rows, rows, tile, tile, P("ty", "tx"), P(), P()),
        out_specs=(tile, tile),
        check_vma=False,
    )
```

```python
import functools

import jax
import jax.numpy as jnp
from jax import lax
from jax.experimental import pallas as pl
from jax.experimental.pallas import tpu as pltpu
from jax.sharding import PartitionSpec as P

BF = jnp.bfloat16
F = jnp.float32
VMEM_LIMIT = 48 * 1024 * 1024
AXES = ("ty", "tx")


def struct(*shape):
    return jax.ShapeDtypeStruct(shape, F)


def iota(shape, dim):
    return lax.broadcasted_iota(jnp.int32, shape, dim)


def mm(a, b, dims=((1,), (0,))):
    return lax.dot_general(a, b, (dims, ((), ())), preferred_element_type=F)


def split3(a):
    hi = a.astype(BF)
    a = a - hi.astype(F)
    mid = a.astype(BF)
    lo = (a - mid.astype(F)).astype(BF)
    return hi, mid, lo


def params():
    return pltpu.CompilerParams(vmem_limit_bytes=VMEM_LIMIT)


def pack_kernel(block, counts_ref, res_ref, out_ref, counts, loaded, built, sems, out_sems, count_sem):
    tiles, slots = res_ref.shape[1:]
    parts = tiles // block
    chunks = slots // 128
    rows = 4 * chunks * block
    take = pltpu.make_async_copy(counts_ref, counts, count_sem)
    take.start()
    loads = [
        pltpu.make_async_copy(res_ref.at[:, pl.ds(i * block, block), :], loaded.at[i], sems.at[i]) for i in range(parts)
    ]
    for load in loads:
        load.start()
    take.wait()
    stores = []
    for i in range(parts):
        loads[i].wait()
        for d in range(0, block, 8):
            live = jnp.zeros((8, 128), jnp.int32)
            for j in range(8):
                live = jnp.where(iota((8, 128), 0) == j, counts[0, i * block + d + j], live)
            for kc in range(chunks):
                keep = iota((8, 128), 1) + 128 * kc < live
                for m in range(4):
                    row = (d * chunks + kc) * 4 + m
                    value = jnp.where(keep, loaded[i, m, d:d + 8, 128 * kc:128 * kc + 128], 0.0)
                    built[i, pl.ds(row, 8, stride=4 * chunks), :] = value
        store = pltpu.make_async_copy(built.at[i], out_ref.at[pl.ds(i * rows, rows), :], out_sems.at[i])
        store.start()
        stores.append(store)
    for store in stores:
        store.wait()


def pack(counts, residual):
    channels, tiles, slots = residual.shape
    block = 32
    parts = tiles // block
    rows = 4 * (slots // 128)
    return pl.pallas_call(
        functools.partial(pack_kernel, block),
        in_specs=[pl.BlockSpec(memory_space=pltpu.HBM)] * 2,
        out_specs=pl.BlockSpec(memory_space=pl.ANY),
        out_shape=struct(tiles * rows, 128),
        scratch_shapes=[
            pltpu.SMEM((1, tiles), jnp.int32),
            pltpu.VMEM((parts, channels, block, slots), F),
            pltpu.VMEM((parts, block * rows, 128), F),
            pltpu.SemaphoreType.DMA((parts,)),
            pltpu.SemaphoreType.DMA((parts,)),
            pltpu.SemaphoreType.DMA,
        ],
        compiler_params=pltpu.CompilerParams(vmem_limit_bytes=62 * 1024 * 1024),
        name="pack_rows",
    )(counts, residual)


def classes_to_diag(kinds, table_ref, level):
    total = jnp.zeros(kinds.shape, F)
    for k in range(table_ref.shape[1]):
        total = jnp.where(kinds == k, table_ref[level, k], total)
    return 4.0 + total


def is_odd(axis):
    return (lax.axis_index(axis) & 1) == 1


def columns_kernel(table_ref, cf_ref, cc_ref, km_ref, with_ref, off_ref, df_ref, dc_ref, square):
    odd = is_odd("tx")
    with_ref[...] = jnp.zeros_like(with_ref)
    off_ref[...] = jnp.zeros_like(off_ref)
    square[...] = jnp.zeros_like(square)
    df = classes_to_diag(km_ref[...], table_ref, 0)
    df_ref[...] = df
    even = km_ref[pl.ds(0, 64, stride=2), :].astype(F).astype(BF)
    pick = jnp.where(iota((128, 128), 0) == 2 * iota((128, 128), 1), 1.0, 0.0).astype(BF)
    dc = classes_to_diag(mm(even, pick).astype(jnp.int32), table_ref, 1)
    dc = jnp.where(iota((64, 128), 1) < 64, dc, 0.0)
    dc_ref[...] = dc

    def send(row, turned, size, width):
        low, high = turned[0:width], turned[size - width:size]
        with_ref[pl.ds(row, width), :] = jnp.where(odd, low, high)
        off_ref[pl.ds(row, width), :] = jnp.where(odd, high, low)

    for m in range(4):
        send(2 * m, cf_ref[m].T, 128, 2)
        square[0:64, 0:64] = cc_ref[m]
        send(8 + 2 * m, square[...].T, 64, 2)
    send(16, df.T, 128, 1)
    square[0:64, :] = dc
    send(17, square[...].T, 64, 1)


def cross(field):
    rows, lanes = field.shape
    near = pltpu.roll(field, 1, 1) + pltpu.roll(field, lanes - 1, 1)
    return near + (pltpu.roll(field, 1, 0) + pltpu.roll(field, rows - 1, 0))


def rows_kernel(
    cf_ref, cc_ref, df_ref, dc_ref, fw_ref, fo_ref, at_ref, with_ref, off_ref, bf_ref, bc_ref, square, vf, wf, vc, wc
):
    odd_x, odd_y = is_odd("tx"), is_odd("ty")
    with_ref[...] = jnp.zeros_like(with_ref)
    off_ref[...] = jnp.zeros_like(off_ref)
    left = jnp.where(odd_x, fw_ref[...], fo_ref[...])
    right = jnp.where(odd_x, fo_ref[...], fw_ref[...])

    def sides(row, first, width):
        square[...] = jnp.zeros_like(square)
        square[first:first + width, :] = right[row:row + width, :]
        square[128 - width:128, :] = left[row:row + width, :]
        return square[...].T

    def send(row, field, size, width):
        lanes = field.shape[1]
        low, high = field[0:width], field[size - width:size]
        with_ref[pl.ds(row, width), 0:lanes] = jnp.where(odd_y, low, high)
        off_ref[pl.ds(row, width), 0:lanes] = jnp.where(odd_y, high, low)

    def twice(field, diag):
        first = jnp.where(diag > 0.0, diag * field - cross(field), 0.0)
        return diag * first - cross(first)

    wf[...] = jnp.zeros_like(wf)
    wf[0:128, 0:128] = df_ref[...]
    wf[0:128, 128:256] = sides(16, 0, 1)
    send(16, wf[...], 128, 1)
    wc[...] = jnp.zeros_like(wc)
    wc[0:64, :] = dc_ref[...] + sides(17, 64, 1)[0:64]
    send(17, wc[...], 64, 1)
    for m in range(4):
        vf[m, 128:136, :] = jnp.zeros((8, 256), F)
        vf[m, 0:128, 0:128] = cf_ref[m]
        vf[m, 0:128, 128:256] = sides(2 * m, 0, 2)
        send(2 * m, vf[m], 128, 2)
        vc[m, 64:72, :] = jnp.zeros((8, 128), F)
        vc[m, 0:64, :] = sides(8 + 2 * m, 64, 2)[0:64]
        vc[m, 0:64, 0:64] = cc_ref[m]
        send(8 + 2 * m, vc[m], 64, 2)
    for m in range(4):
        bf_ref[m] = twice(vf[m], wf[...])[0:128, 0:128]
        bc_ref[m] = twice(vc[m], wc[...])[0:64, :]


def rim(own, other, rows, diag, lanes, step):
    here = own[diag:diag + 1, 0:lanes]
    there = other[diag:diag + 1, 0:lanes]
    near = other[rows:rows + 8, 0:lanes]
    far = pltpu.roll(near, step, 0)
    edge = pltpu.roll(own[rows:rows + 8, 0:lanes], step, 0)

    def sideways(x):
        return pltpu.roll(x, 1, 1) + pltpu.roll(x, lanes - 1, 1)

    change = jnp.where(here > 0.0, -near, 0.0)
    beyond = jnp.where(there > 0.0, there * near - (far + edge + sideways(near)), 0.0)
    return here * change - sideways(change) - beyond, -change


def finish_kernel(
    lw_ref, acc, bf_ref, bc_ref, with_ref, off_ref, fw_ref, fo_ref, fine_ref, coarse_ref,
    lw, tall, low, fine_out, coarse_out, sems, lw_sem,
):
    take = pltpu.make_async_copy(lw_ref, lw, lw_sem)
    take.start()
    a = iota((256, 256), 0)
    b = iota((256, 256), 1)
    place = ((b >> 7) == ((a >> 5) & 1)) & ((b & 127) == 1 + 4 * (a & 31) + (a >> 6))
    place = jnp.where(place, 1.0, 0.0).astype(BF)
    wide = sum(mm(p, place) for p in split3(acc[...]))
    far = jnp.abs(iota((128, 128), 0) - 2 * iota((128, 128), 1))
    halve = jnp.where(far == 0, 0.75, jnp.where(far == 1, 0.5, jnp.where(far == 2, 0.125, 0.0))).astype(BF)

    def edges(out, m, size, width, above, below):
        for row, (both, at) in ((0, (above, 2 * m + 1)), (size - 1, (below, 2 * m))):
            inner = 1 if row == 0 else size - 2
            out[m, row:row + 1, :] = out[m, row:row + 1, :] - both[0][at:at + 1, 0:width]
            out[m, inner:inner + 1, :] = out[m, inner:inner + 1, :] - both[1][at:at + 1, 0:width]

    odd = is_odd("ty")
    top = jnp.where(odd, with_ref[...], off_ref[...])
    bottom = jnp.where(odd, off_ref[...], with_ref[...])
    before = jnp.where(odd, fw_ref[...], fo_ref[...])
    after = jnp.where(odd, fo_ref[...], fw_ref[...])
    above = rim(top, before, 0, 16, 256, 1)
    below = rim(bottom, after, 0, 16, 256, 7)
    coarse_above = rim(top, before, 8, 17, 128, 1)
    coarse_below = rim(bottom, after, 8, 17, 128, 7)
    take.wait()
    sends = []
    for m in range(4):
        tall[m, 0:16, :] = jnp.zeros((16, 128), F)
        tall[m, 72:144, :] = jnp.zeros((72, 128), F)
        for h in range(2):
            for r in range(4):
                at = m * 64 + r * 16
                spots = pl.ds(9 + 61 * h + r, 16, stride=4)
                part = wide[at:at + 16, h * 128:(h + 1) * 128]
                tall[m, spots, :] = part if h == 0 else part + tall[m, spots, :]
        every = [tall[m, pl.ds(8 + k, 64, stride=2), :] for k in range(-2, 3)]
        low[m * 64:(m + 1) * 64, :] = 0.75 * every[2] + 0.5 * (every[1] + every[3]) + 0.125 * (every[0] + every[4])
        fine_out[m] = lw[0] * tall[m, 8:136, :] - bf_ref[m]
        edges(fine_out, m, 128, 128, above, below)
        send = pltpu.make_async_copy(fine_out.at[m], fine_ref.at[m], sems.at[m])
        send.start()
        sends.append(send)
    coarse = sum(mm(p, halve) for p in split3(low[...]))
    for m in range(4):
        coarse_out[m] = lw[1] * coarse[m * 64:(m + 1) * 64, 0:64] - bc_ref[m, :, 0:64]
        edges(coarse_out, m, 64, 64, coarse_above, coarse_below)
    send = pltpu.make_async_copy(coarse_out, coarse_ref, sems.at[4])
    send.start()
    for send in sends + [send]:
        send.wait()


def swap(x, axis, first):
    pairs = [(i, i + 1) for i in range(first, lax.axis_size(axis) - 1, 2)]
    return lax.ppermute(x, axis, pairs + [(j, i) for i, j in pairs])


def edges(coef_fine, coef_coarse, kappa_map, kappa_table, at):
    smem = pl.BlockSpec(memory_space=pltpu.SMEM)
    vmem = pl.BlockSpec(memory_space=pltpu.VMEM)
    square = pltpu.VMEM((128, 128), F)
    with_x, off_x, df, dc = pl.pallas_call(
        columns_kernel,
        in_specs=[smem] + [vmem] * 3,
        out_shape=[struct(24, 128), struct(24, 128), struct(128, 128), struct(64, 128)],
        scratch_shapes=[square],
        compiler_params=params(),
        name="edge_columns",
    )(kappa_table, coef_fine, coef_coarse, kappa_map)
    from_with = swap(with_x, "tx", 0)
    from_off = swap(off_x, "tx", 1)
    with_y, off_y, fine, coarse = pl.pallas_call(
        rows_kernel,
        in_specs=[vmem] * 6 + [pl.BlockSpec(memory_space=pl.ANY)],
        out_shape=[struct(24, 256), struct(24, 256), struct(4, 128, 128), struct(4, 64, 128)],
        scratch_shapes=[
            square,
            pltpu.VMEM((4, 136, 256), F),
            pltpu.VMEM((136, 256), F),
            pltpu.VMEM((4, 72, 128), F),
            pltpu.VMEM((72, 128), F),
        ],
        compiler_params=params(),
        name="edge_rows",
    )(coef_fine, coef_coarse, df, dc, from_with, from_off, at)
    return fine, coarse, with_y, off_y, swap(with_y, "ty", 0), swap(off_y, "ty", 1)


def finish(level_weight, total, fields):
    vmem = pl.BlockSpec(memory_space=pltpu.VMEM)
    return pl.pallas_call(
        finish_kernel,
        in_specs=[pl.BlockSpec(memory_space=pl.ANY)] + [vmem] * (1 + len(fields)),
        out_specs=[pl.BlockSpec(memory_space=pl.ANY)] * 2,
        out_shape=[struct(4, 128, 128), struct(4, 64, 64)],
        scratch_shapes=[
            pltpu.SMEM((2,), F),
            pltpu.VMEM((4, 144, 128), F),
            pltpu.VMEM((256, 128), F),
            pltpu.VMEM((4, 128, 128), F),
            pltpu.VMEM((4, 64, 64), F),
            pltpu.SemaphoreType.DMA((5,)),
            pltpu.SemaphoreType.DMA,
        ],
        compiler_params=params(),
        name="finish_tiles",
    )(level_weight, total, *fields)


def spline(t):
    s = 1.0 - t
    return (
        s * s * s / 6.0,
        (3.0 * t * t * t - 6.0 * t * t + 4.0) / 6.0,
        (-3.0 * t * t * t + 3.0 * t * t + 3.0 * t + 1.0) / 6.0,
        t * t * t / 6.0,
    )


def rotate(weights, start):
    odd = (start & 1) == 1
    weights = [jnp.where(odd, weights[(r - 1) % 4], weights[r]) for r in range(4)]
    two = (start & 2) == 2
    return [jnp.where(two, weights[(r - 2) % 4], weights[r]) for r in range(4)]


def place_kernel(off_ref, pos_ref, out_ref):
    sy = off_ref[0] - 2
    sx = off_ref[1] - 2
    upper = sy >= 61
    sy = jnp.where(upper, sy - 61, sy)
    by = sy & 3
    bx = sx & 3
    qy = sy >> 2
    qx = (sx >> 2) + jnp.where(upper, 32, 0)
    wy = rotate(spline(pos_ref[0]), by)
    wx = rotate(spline(pos_ref[1]), bx)
    for r in range(4):
        out_ref[r] = (qy + jnp.where(by > r, 1, 0)).astype(F)
        out_ref[4 + r] = (qx + jnp.where(bx > r, 1, 0)).astype(F)
        out_ref[8 + r] = wx[r]
        out_ref[12 + r] = wy[r]


def places(offsets, positions):
    tiles, slots = offsets.shape[1:]
    group = 16
    points = pl.BlockSpec((2, group, slots), lambda i: (0, i, 0))
    return pl.pallas_call(
        place_kernel,
        grid=(tiles // group,),
        in_specs=[points, points],
        out_specs=pl.BlockSpec((16, group, slots), lambda i: (0, i, 0)),
        out_shape=struct(16, tiles, slots),
        compiler_params=params(),
        name="place_rows",
    )(offsets, positions)


def project_kernel(group, slots, v_ref, at_ref, acc, values):
    @pl.when(pl.program_id(0) == 0)
    def _():
        acc[...] = jnp.zeros_like(acc)

    chunks = slots // 128
    base = pl.multiple_of(pl.program_id(0) * (group * 4 * chunks), group * 4 * chunks)

    def weigh(first, m):
        rows = [v_ref[pl.ds(base + (first * chunks + kc) * 4 + m, 8, stride=4 * chunks), :] for kc in range(chunks)]
        v = jnp.concatenate(rows, 1)
        for r in range(4):
            values[4 * m + r, first:first + 8, :] = v * at_ref[12 + r, first:first + 8, :]

    for m in range(4):
        weigh(0, m)
    i16 = iota((16, slots), 0).astype(F).astype(BF)
    i64 = iota((64, slots), 0).astype(F).astype(BF)
    zero = jnp.zeros((), BF)

    def spread(ref, i, s, n):
        row = jnp.broadcast_to(ref[i, pl.ds(s, 1), :], (16, slots)).astype(BF)
        return jnp.broadcast_to(row[None], (n // 16, 16, slots)).reshape(n, slots)

    def build(s):
        left = [None] * 16
        for r in range(4):
            here = i16 == spread(at_ref, r, s, 16)
            for m in range(4):
                left[4 * m + r] = jnp.where(here, spread(values, 4 * m + r, s, 16), zero)
        right = [jnp.where(i64 == spread(at_ref, 4 + r, s, 64), spread(at_ref, 8 + r, s, 64), zero) for r in range(4)]
        return jnp.concatenate(left, 0), jnp.concatenate(right, 0)

    held = []
    for s in range(group):
        if s + 8 < group and s % 2 == 1:
            weigh(s // 8 * 8 + 8, s % 8 // 2)
        held.append(build(s))
        if len(held) == 4:
            left, right = (jnp.concatenate(side, 1) for side in zip(*held))
            acc[...] += mm(left, right, ((1,), (1,)))
            held.clear()


def project(values, at):
    tiles, slots = at.shape[1:]
    group = 32
    return pl.pallas_call(
        functools.partial(project_kernel, group, slots),
        grid=(tiles // group,),
        in_specs=[
            pl.BlockSpec(memory_space=pltpu.VMEM),
            pl.BlockSpec((16, group, slots), lambda i: (0, i, 0)),
        ],
        out_specs=pl.BlockSpec((256, 256), lambda i: (0, 0)),
        out_shape=struct(256, 256),
        scratch_shapes=[pltpu.VMEM((16, group, slots), F)],
        compiler_params=params(),
        name="project_rows",
    )(values, at)


def on_device(residual, counts, offsets, positions, coef_fine, coef_coarse, kappa_map, kappa_table, level_weight):
    tiles = residual.shape[2]
    packed = pack(counts, residual[0]).reshape(tiles, -1, 4, 128)
    values = lax.all_to_all(packed, AXES, split_axis=0, concat_axis=0, tiled=True).reshape(-1, 128)
    at = places(offsets[0], positions[0])
    fields = edges(coef_fine, coef_coarse, kappa_map, kappa_table, at)
    return tuple(finish(level_weight, project(values, at), fields))


def solution(mesh):
    rows = P(AXES, None, None, None)
    tile = P(None, "ty", "tx")
    return jax.shard_map(
        on_device,
        mesh=mesh,
        in_specs=(rows, P(AXES, None), rows, rows, tile, tile, P("ty", "tx"), P(), P()),
        out_specs=(tile, tile),
        check_vma=False,
    )
```
